32 devices in a mesh: ctx: 8 (over z, x), kvh: 4 (over y, core).
Axes of the slice: x: 2, y: 2, z: 4, core: 2. Of those that a mesh axis runs over, the one named last changes fastest.
Arguments:
- queries: bfloat16 [8192, 8192], P('ctx', 'kvh'), may hold values from -8 to 8
- keys: bfloat16 [8192, 1024], P(('ctx', 'kvh')), may hold values from -8 to 8
- values: bfloat16 [8192, 1024], P(('ctx', 'kvh')), may hold values from -6 to 6
- out_grad: bfloat16 [8192, 8192], P('ctx', 'kvh'), may hold values from -6 to 6
- random_blocks: int32 [64, 3], replicated, may hold values from 8 to 63, as said below
Outputs:
- attended: bfloat16 [8192, 8192], P('ctx', 'kvh')
- query_grad: bfloat16 [8192, 8192], P('ctx', 'kvh')
- key_grad: bfloat16 [8192, 1024], P(('ctx', 'kvh'))
- value_grad: bfloat16 [8192, 1024], P(('ctx', 'kvh'))
The draws below stay inside these ranges and needn't reach their ends.
Inputs may be any that keep to these rules, and one draw needn't show every extreme that they name: `random_blocks`: block b lies on ctx index b // 8. For each query block the 3 named blocks lie on 3 different ctx indices, none of them 0, the index holding the query block, or its two neighbours. Over the 8 rows of one ctx index, the named blocks (repeats counted) fall on 4 ctx indices as evenly as possible: none holds more than 6 of them and some holds exactly 6.
All inputs are finite; a program needn't handle non-finite values.
Results may differ from the reference program's by a relative error of at most 0.014.
Values may be sent and summed in bfloat16 or wider, within the bound.
No kernel may reach another device: no remote copies, remote signals or barrier semaphores. Data moves between devices by JAX's collectives and lax.ppermute only.
A program may use at most 128 MiB of HBM per device.

```python
import math
import jax
import jax.numpy as jnp
from jax import lax

HD = 128
QPK = 8
KVH = 8
BLK = 128
GLOB = 2
RAND = 3
HEADS = 64
TOKENS = 8192
NKB = 64
QB_DEV = 8


def scale_rows(subkey, count_rows, count_cols):
    log_low = math.log(0.35)
    log_high = math.log(3.0)
    return jnp.exp(jax.random.uniform(subkey, (count_rows, count_cols, 1), jnp.float32, log_low, log_high))


def draw_queries(key, part):
    row_scales = scale_rows(jax.random.fold_in(key, 11), TOKENS, HEADS)
    entries = jax.random.normal(jax.random.fold_in(key, 13), (TOKENS, HEADS, HD), jnp.float32) * row_scales
    return jnp.clip(entries, -8.0, 8.0).reshape(TOKENS, HEADS * HD).astype(jnp.bfloat16)


def draw_keys(key, part):
    row_scales = scale_rows(jax.random.fold_in(key, 21), TOKENS, KVH)
    entries = jax.random.normal(jax.random.fold_in(key, 23), (TOKENS, KVH, HD), jnp.float32) * row_scales
    return jnp.clip(entries, -8.0, 8.0).reshape(TOKENS, KVH * HD).astype(jnp.bfloat16)


def shuffled(subkey, devices):
    return jax.random.permutation(subkey, devices)


def draw_random_blocks(key, part):
    devices = NKB // QB_DEV
    far_count = devices - 4
    slot_count = QB_DEV * RAND
    order_keys = jax.random.split(jax.random.fold_in(key, 31), devices)
    ranking = jax.vmap(lambda subkey: shuffled(subkey, devices))(order_keys)
    device_ids = jnp.arange(devices)
    nearby = (device_ids[None, :] == 0) | (jnp.abs(device_ids[None, :] - device_ids[:, None]) <= 1)
    scores = jnp.where(nearby, ranking + devices, ranking)
    ordering = jnp.argsort(scores, axis=1, stable=True)
    far_list = ordering[:, :far_count]
    slot_ids = jnp.arange(slot_count) % far_count
    owners = far_list[:, slot_ids]
    offsets = jax.random.randint(jax.random.fold_in(key, 32), (devices, slot_count), 0, QB_DEV)
    return (owners * QB_DEV + offsets).astype(jnp.int32).reshape(NKB, RAND)


def block_scale(stream_key, shape, cuts, low, top_value):
    def one(axis_at, shards_of):
        heights = jax.random.uniform(jax.random.fold_in(jax.random.fold_in(stream_key, 6), axis_at), (shards_of,), jnp.float32, low / len(cuts), top_value / len(cuts))
        return jnp.repeat(jnp.exp(heights), shape[axis_at] // shards_of).reshape((-1,) + (1,) * (len(shape) - axis_at - 1))

    gain = one(*cuts[0])
    for cut in cuts[1:]:
        gain = gain * one(*cut)
    return gain


def centred(rng, shape, deviation, reach, pieces=(), kind=jnp.bfloat16):
    factor_of = block_scale(rng, shape, pieces, -0.22, 0.18) if pieces else 1.0
    result = jax.random.normal(rng, shape, jnp.float32) * deviation * factor_of
    return jnp.minimum(jnp.maximum(result, -reach), reach).astype(kind)


def setup_inputs(seed: int = 0) -> dict:
    seeds = jax.random.split(jax.random.key(seed), 6)
    return {
        "queries": draw_queries(jax.random.fold_in(seeds[5], 71), 0),
        "keys": draw_keys(jax.random.fold_in(seeds[5], 71), 0),
        "values": centred(seeds[2], (TOKENS, KVH * HD), 1.0, 6.0, ((0, 32),)),
        "out_grad": centred(seeds[3], (TOKENS, HEADS * HD), 1.0, 6.0, ((0, 8), (1, 4))),
        "random_blocks": draw_random_blocks(jax.random.fold_in(seeds[5], 71), 0),
    }


def reference(queries, keys, values, out_grad, random_blocks):
    tokens = queries.shape[0]
    all_blocks = tokens // BLK
    score_scale = HD ** -0.5
    select_count = 3 + GLOB + RAND
    query_rows = queries.reshape(all_blocks, BLK, KVH, QPK, HD)
    grad_rows = out_grad.reshape(all_blocks, BLK, KVH, QPK, HD)
    key_blocks = keys.reshape(all_blocks, BLK, KVH, HD)
    value_blocks = values.reshape(all_blocks, BLK, KVH, HD)

    def visit_block(accums, step_items):
        key_acc, value_acc = accums
        block_index, query_here, grad_here, chosen = step_items
        window_ids = block_index - 1 + jnp.arange(3, dtype=jnp.int32)
        listed = jnp.concatenate([window_ids, jnp.arange(GLOB, dtype=jnp.int32), chosen.astype(jnp.int32)])
        usable = jnp.concatenate([(window_ids >= GLOB) & (window_ids < all_blocks), jnp.ones((GLOB + RAND,), jnp.bool_)])
        usable = jnp.repeat(usable, BLK)
        listed = jnp.clip(listed, 0, all_blocks - 1).astype(jnp.int32)
        key_rows = key_blocks[listed].reshape(select_count * BLK, KVH, HD).astype(jnp.float32)
        value_rows = value_blocks[listed].reshape(select_count * BLK, KVH, HD).astype(jnp.float32)
        query_f = query_here.astype(jnp.float32)
        grad_f = grad_here.astype(jnp.float32)
        scores = jnp.einsum("bgqd,kgd->gqbk", query_f, key_rows) * score_scale
        scores = jnp.where(usable, scores, -jnp.inf)
        largest = jnp.max(scores, axis=-1, keepdims=True)
        raised = jnp.exp(scores - largest)
        probs = raised / jnp.sum(raised, axis=-1, keepdims=True)
        weights = lax.optimization_barrier(probs.astype(jnp.bfloat16)).astype(jnp.float32)
        attended = jnp.einsum("gqbk,kgd->bgqd", weights, value_rows)
        prob_grad = jnp.einsum("bgqd,kgd->gqbk", grad_f, value_rows)
        centre = jnp.sum(probs * prob_grad, axis=-1, keepdims=True)
        score_grad = lax.optimization_barrier((probs * (prob_grad - centre) * score_scale).astype(jnp.bfloat16)).astype(jnp.float32)
        query_grad = jnp.einsum("gqbk,kgd->bgqd", score_grad, key_rows)
        key_grad = jnp.einsum("gqbk,bgqd->kgd", score_grad, query_f)
        value_grad = jnp.einsum("gqbk,bgqd->kgd", weights, grad_f)
        key_acc = key_acc.at[listed].add(key_grad.reshape(select_count, BLK, KVH, HD))
        value_acc = value_acc.at[listed].add(value_grad.reshape(select_count, BLK, KVH, HD))
        return (key_acc, value_acc), (attended.astype(jnp.bfloat16), query_grad.astype(jnp.bfloat16))

    zeros_acc = jnp.zeros((all_blocks, BLK, KVH, HD), jnp.float32)
    block_list = jnp.arange(all_blocks, dtype=jnp.int32)
    (key_acc, value_acc), (attended, query_grad) = lax.scan(visit_block, (zeros_acc, zeros_acc), (block_list, query_rows, grad_rows, random_blocks))
    return (attended.reshape(tokens, KVH * QPK * HD), query_grad.reshape(tokens, KVH * QPK * HD), key_acc.reshape(tokens, KVH * HD).astype(jnp.bfloat16), value_acc.reshape(tokens, KVH * HD).astype(jnp.bfloat16))
```

```python
import functools

import jax
import jax.numpy as jnp
from jax import lax
from jax.experimental import pallas as pl
from jax.experimental.pallas import tpu as pltpu
from jax.sharding import PartitionSpec as P

HD = 128
BLK = 128
GLOB = 2
DEPTH = 4
LOG2E = 1.4426950408889634
NN = (((1,), (0,)), ((), ()))
NT = (((1,), (1,)), ((), ()))
VMEM_LIMIT = 56 * 1024 * 1024


class Plan:
    def __init__(self, ctx, query_blocks, rand):
        self.ctx, self.qb, self.rand = ctx, query_blocks, rand
        self.depth = DEPTH if ctx % DEPTH == 0 else ctx
        self.lanes = ctx // self.depth
        named = query_blocks * rand
        per_owner = -(-named // max(1, ctx - 4))
        most = 0
        for device in range(ctx):
            far = [s for s in range(1, ctx) if abs(s - device) > 1]
            for lane in range(self.lanes):
                if lane != device % self.lanes:
                    most = max(most, sum(s % self.lanes == lane for s in far))
        self.slots = 2 + GLOB + min(named, per_owner * most)
        self.own = self.depth * query_blocks
        self.pool = self.own + (self.lanes - 1) * self.slots

    def column_place(self, me, owner, offset):
        row = lax.rem(me // self.lanes - owner // self.lanes + self.depth, self.depth)
        return row * self.qb + offset

    def place(self, me, owner, offset, slot):
        mine, theirs = lax.rem(me, self.lanes), lax.rem(owner, self.lanes)
        pack = lax.rem(theirs - mine + self.lanes, self.lanes) - 1
        return jnp.where(
            mine == theirs, self.column_place(me, owner, offset), self.own + pack * self.slots + slot
        )


def dot(a, b, dims):
    return lax.dot_general(a, b, dims, preferred_element_type=jnp.float32)


def fill_table(plan, me, named, table, counts):
    qb, rand, lanes = plan.qb, plan.rand, plan.lanes
    sel = 3 + GLOB + rand
    left, right = jnp.maximum(me - 1, 0), jnp.minimum(me + 1, plan.ctx - 1)
    for lane in range(lanes):
        counts[lane] = 2 + GLOB
    for i in range(qb):
        table[i * sel] = plan.place(me, left, qb - 1, 0) if i == 0 else jnp.int32(i - 1)
        table[i * sel + 1] = jnp.int32(i)
        table[i * sel + 2] = plan.place(me, right, 0, 1) if i == qb - 1 else jnp.int32(i + 1)
        for j in range(GLOB):
            table[i * sel + 3 + j] = plan.place(me, jnp.int32(0), j, 2 + j)

    def entry(n, carry):
        block = named[me * (qb * rand) + n]
        owner = block // qb
        lane = lax.rem(owner, lanes)
        slot = counts[lane]
        table[(n // rand) * sel + 3 + GLOB + lax.rem(n, rand)] = plan.place(
            me, owner, lax.rem(block, qb), slot
        )
        counts[lane] = slot + 1
        return carry

    lax.fori_loop(0, qb * rand, entry, 0)


def walk_pack(plan, me, other, named, visit):
    qb, rand, lanes = plan.qb, plan.rand, plan.lanes
    mine = lax.rem(me, lanes)

    @pl.when((other >= 1) & (lax.rem(other - 1 + lanes, lanes) == mine))
    def _():
        visit(0, plan.column_place(me, other - 1, qb - 1))

    @pl.when((other + 1 < plan.ctx) & (lax.rem(other + 1, lanes) == mine))
    def _():
        visit(1, plan.column_place(me, other + 1, 0))

    @pl.when(mine == 0)
    def _():
        for j in range(GLOB):
            visit(2 + j, plan.column_place(me, jnp.int32(0), j))

    def entry(n, slot):
        block = named[other * (qb * rand) + n]
        owner = block // qb
        hit = lax.rem(owner, lanes) == mine

        @pl.when(hit)
        def _():
            visit(slot, plan.column_place(me, owner, lax.rem(block, qb)))

        return slot + hit.astype(jnp.int32)

    lax.fori_loop(0, qb * rand, entry, jnp.int32(2 + GLOB))


def rows_of(place):
    return pl.ds(pl.multiple_of(place * BLK, BLK), BLK)


def pack_kernel(where, named, *refs, plan, step):
    shards, out = refs[: plan.depth], refs[plan.depth]
    me = where[0]
    lane = lax.rem(me, plan.lanes)
    other = me - lane + lax.rem(lane + step, plan.lanes)
    rows = plan.qb * BLK
    out[...] = jnp.zeros_like(out)

    def visit(slot, place):
        at = lax.rem(place, plan.qb)
        for k in range(plan.depth):

            @pl.when(place // plan.qb == k)
            def _():
                out[rows_of(slot), :] = shards[k][rows_of(at), :]

    walk_pack(plan, me, other, named, visit)


def pack(plan, where, named, shards, step):
    rows = plan.qb * BLK
    return pl.pallas_call(
        functools.partial(pack_kernel, plan=plan, step=step),
        grid_spec=pltpu.PrefetchScalarGridSpec(
            num_scalar_prefetch=2,
            grid=(1,),
            in_specs=[pl.BlockSpec((rows, HD), lambda n, *_: (0, 0))] * plan.depth,
            out_specs=pl.BlockSpec((plan.slots * BLK, HD), lambda n, *_: (0, 0)),
        ),
        out_shape=jax.ShapeDtypeStruct((plan.slots * BLK, HD), jnp.bfloat16),
        compiler_params=pltpu.CompilerParams(vmem_limit_bytes=VMEM_LIMIT),
        cost_estimate=pl.CostEstimate(flops=0, bytes_accessed=4 << 20, transcendentals=0),
        name="pack_blocks",
    )(where, named, *shards)


def merge_kernel(where, named, column, *refs, plan):
    packs, outs, total = refs[: plan.lanes - 1], refs[plan.lanes - 1 : -1], refs[-1]
    me = where[0]
    lane = lax.rem(me, plan.lanes)
    total[...] = column[...]
    for step in range(1, plan.lanes):
        other = me - lane + lax.rem(lane + step, plan.lanes)

        def visit(slot, place):
            total[rows_of(place), :] += packs[step - 1][rows_of(slot), :].astype(jnp.float32)

        walk_pack(plan, me, other, named, visit)
    rows = plan.qb * BLK
    for k in range(plan.depth):
        outs[k][...] = total[k * rows : (k + 1) * rows, :].astype(outs[k].dtype)


def merge(plan, where, named, column, packs):
    rows = plan.qb * BLK
    kinds = [jnp.float32] + [jnp.bfloat16] * (plan.depth - 1)
    return pl.pallas_call(
        functools.partial(merge_kernel, plan=plan),
        grid_spec=pltpu.PrefetchScalarGridSpec(
            num_scalar_prefetch=2,
            grid=(1,),
            in_specs=[pl.BlockSpec((plan.own * BLK, HD), lambda n, *_: (0, 0))]
            + [pl.BlockSpec((plan.slots * BLK, HD), lambda n, *_: (0, 0))] * len(packs),
            out_specs=[pl.BlockSpec((rows, HD), lambda n, *_: (0, 0))] * plan.depth,
            scratch_shapes=[pltpu.VMEM((plan.own * BLK, HD), jnp.float32)],
        ),
        out_shape=[jax.ShapeDtypeStruct((rows, HD), kind) for kind in kinds],
        compiler_params=pltpu.CompilerParams(vmem_limit_bytes=VMEM_LIMIT),
        cost_estimate=pl.CostEstimate(flops=0, bytes_accessed=6 << 20, transcendentals=0),
        name="merge_terms",
    )(where, named, column, *packs)


def attend_kernel(where, named, *refs, plan, qpk, per):
    parts = plan.depth + plan.lanes - 1
    q_ref, do_ref = refs[:2]
    k_parts, v_parts = refs[2 : 2 + parts], refs[2 + parts : 2 + 2 * parts]
    refs = refs[2 + 2 * parts :]
    o_ref, dq_ref, dk_col, dv_col = refs[:4]
    dk_packs, dv_packs = refs[4 : 3 + plan.lanes], refs[3 + plan.lanes : 2 + 2 * plan.lanes]
    kpool, vpool, keys, values, dk_sum, dv_sum, dk_far, dv_far, table, counts = refs[2 + 2 * plan.lanes :]
    me = where[0]
    i = pl.program_id(0)
    rows = plan.qb * BLK
    sel = 3 + GLOB + plan.rand
    scale = HD ** -0.5

    @pl.when(i == 0)
    def _():
        fill_table(plan, me, named, table, counts)
        for pool, given in ((kpool, k_parts), (vpool, v_parts)):
            at = 0
            for part in given:
                pool[at : at + part.shape[0], :] = part[...]
                at += part.shape[0]
        for total in (dk_col, dv_col, dk_far, dv_far):
            total[...] = jnp.zeros_like(total)

    for j in range(sel):
        place = rows_of(table[i * sel + j])
        keys[j * BLK : (j + 1) * BLK, :] = kpool[place, :]
        values[j * BLK : (j + 1) * BLK, :] = vpool[place, :]
    block = me * plan.qb + i
    counted = [(block - 1 + j >= GLOB) & (block - 1 + j < plan.ctx * plan.qb) for j in range(3)]
    K, V = keys[...], values[...]
    KT, VT = K.T, V.T
    for h in range(0, qpk, per):

        def stacked(ref):
            return jnp.concatenate([ref[:, (h + t) * HD : (h + t + 1) * HD] for t in range(per)], axis=0)

        q, do = stacked(q_ref), stacked(do_ref)
        scores = dot(K, q, NT)
        scores = jnp.concatenate(
            [jnp.where(counted[j], scores[j * BLK : (j + 1) * BLK], -jnp.inf) for j in range(3)]
            + [scores[3 * BLK :]],
            axis=0,
        )
        largest = jnp.max(scores, axis=0, keepdims=True)
        raised = jnp.exp2((scores - largest) * (scale * LOG2E))
        inverse = 1.0 / jnp.sum(raised, axis=0, keepdims=True)
        raised_b = raised.astype(jnp.bfloat16)
        attended = dot(VT, raised_b, NN) * inverse
        prob_grad = dot(V, do, NT)
        do_t, q_t = do.T.astype(jnp.float32), q.T.astype(jnp.float32)
        centre = jnp.sum(attended * do_t, axis=0, keepdims=True)
        score_grad = (raised * (prob_grad - centre)).astype(jnp.bfloat16)
        query_grad = dot(KT, score_grad, NN) * (inverse * scale)
        value_grad = dot(raised_b, (do_t * inverse).astype(jnp.bfloat16), NT)
        key_grad = dot(score_grad, (q_t * (inverse * scale)).astype(jnp.bfloat16), NT)
        attended, query_grad = attended.T, query_grad.T
        for t in range(per):
            o_ref[:, (h + t) * HD : (h + t + 1) * HD] = attended[t * BLK : (t + 1) * BLK].astype(jnp.bfloat16)
            dq_ref[:, (h + t) * HD : (h + t + 1) * HD] = query_grad[t * BLK : (t + 1) * BLK].astype(jnp.bfloat16)
        if h == 0:
            dk_sum[...], dv_sum[...] = key_grad, value_grad
        else:
            dk_sum[...] += key_grad
            dv_sum[...] += value_grad
    for j in range(sel):
        place = table[i * sel + j]
        part = slice(j * BLK, (j + 1) * BLK)

        @pl.when(place < plan.own)
        def _():
            dk_col[rows_of(place), :] += dk_sum[part, :]
            dv_col[rows_of(place), :] += dv_sum[part, :]

        @pl.when(place >= plan.own)
        def _():
            dk_far[rows_of(place - plan.own), :] += dk_sum[part, :]
            dv_far[rows_of(place - plan.own), :] += dv_sum[part, :]

    @pl.when(i == pl.num_programs(0) - 1)
    def _():
        size = plan.slots * BLK
        for n in range(plan.lanes - 1):
            dk_packs[n][...] = dk_far[n * size : (n + 1) * size, :].astype(jnp.bfloat16)
            dv_packs[n][...] = dv_far[n * size : (n + 1) * size, :].astype(jnp.bfloat16)


def attend(plan, where, named, queries, out_grad, k_parts, v_parts, group, qpk):
    width = qpk * HD
    sel = 3 + GLOB + plan.rand
    far = (plan.lanes - 1) * plan.slots * BLK
    whole = lambda a: pl.BlockSpec(a.shape, lambda n, *_: (0, 0))
    q_spec = pl.BlockSpec((BLK, width), lambda n, *_: (n, group))
    o_spec = pl.BlockSpec((BLK, width), lambda n, *_: (n, 0))
    o_shape = jax.ShapeDtypeStruct((plan.qb * BLK, width), jnp.bfloat16)
    column = jax.ShapeDtypeStruct((plan.own * BLK, HD), jnp.float32)
    packed = jax.ShapeDtypeStruct((plan.slots * BLK, HD), jnp.bfloat16)
    out_shape = [o_shape, o_shape, column, column] + [packed] * (2 * (plan.lanes - 1))
    pairs = plan.qb * qpk * BLK * sel * BLK
    out = pl.pallas_call(
        functools.partial(attend_kernel, plan=plan, qpk=qpk, per=4 if qpk % 4 == 0 else 1),
        grid_spec=pltpu.PrefetchScalarGridSpec(
            num_scalar_prefetch=2,
            grid=(plan.qb,),
            in_specs=[q_spec, q_spec] + [whole(a) for a in k_parts] + [whole(a) for a in v_parts],
            out_specs=[o_spec, o_spec] + [whole(s) for s in out_shape[2:]],
            scratch_shapes=[
                pltpu.VMEM((plan.pool * BLK, HD), jnp.bfloat16),
                pltpu.VMEM((plan.pool * BLK, HD), jnp.bfloat16),
                pltpu.VMEM((sel * BLK, HD), jnp.bfloat16),
                pltpu.VMEM((sel * BLK, HD), jnp.bfloat16),
                pltpu.VMEM((sel * BLK, HD), jnp.float32),
                pltpu.VMEM((sel * BLK, HD), jnp.float32),
                pltpu.VMEM((far, HD), jnp.float32),
                pltpu.VMEM((far, HD), jnp.float32),
                pltpu.SMEM((plan.qb * sel,), jnp.int32),
                pltpu.SMEM((plan.lanes,), jnp.int32),
            ],
        ),
        out_shape=out_shape,
        compiler_params=pltpu.CompilerParams(vmem_limit_bytes=VMEM_LIMIT),
        cost_estimate=pl.CostEstimate(
            flops=12 * pairs * HD, bytes_accessed=24 << 20, transcendentals=pairs
        ),
        name="attend_head",
    )(where, named, queries, out_grad, *k_parts, *v_parts)
    return out[0], out[1], out[2:4], (out[4 : 3 + plan.lanes], out[3 + plan.lanes :])


def column_shift(array, plan, rows):
    return lax.ppermute(array, "ctx", [(n, (n + rows * plan.lanes) % plan.ctx) for n in range(plan.ctx)])


def row_shift(array, plan, lanes):
    return lax.ppermute(
        array, "ctx", [(n, n - n % plan.lanes + (n + lanes) % plan.lanes) for n in range(plan.ctx)]
    )


def after(array, *others):
    return lax.optimization_barrier((array, *others))[0]


def per_device(queries, keys, values, out_grad, random_blocks):
    stacked = jnp.stack([keys, values])
    local_kv = lax.all_to_all(stacked, "kvh", split_axis=2, concat_axis=1, tiled=True)
    tok_rows = local_kv.shape[1]
    groups = local_kv.shape[2] // HD
    qpk = queries.shape[1] // (groups * HD)
    plan = Plan(lax.axis_size("ctx"), tok_rows // BLK, random_blocks.shape[1])
    lanes, depth = plan.lanes, plan.depth
    where = lax.axis_index("ctx").astype(jnp.int32).reshape(1)
    named = random_blocks.reshape(-1)

    parts, waits = [], []
    for g in range(groups):
        both = []
        for n in range(2):
            own = local_kv[n, :, g * HD : (g + 1) * HD]
            if g:
                own = after(own, *waits)
            shards = [own] + [column_shift(own, plan, k) for k in range(1, depth)]
            both.append(shards)
        waits = both[0][1:] + both[1][1:]
        for shards in both:
            packs = [row_shift(pack(plan, where, named, shards[:depth], lanes - t), plan, lanes - t) for t in range(1, lanes)]
            shards.extend(packs)
        parts.append(both)

    attended, query_grad, grads = [], [], []
    for g in range(groups):
        o, dq, columns, packs = attend(plan, where, named, queries, out_grad, *parts[g], g, qpk)
        attended.append(o)
        query_grad.append(dq)
        for column, far in zip(columns, packs):
            back = [row_shift(far[t - 1], plan, t) for t in range(1, lanes)]
            shards = merge(plan, where, named, column, back[::-1])
            total = shards[0]
            for k in range(1, depth):
                total = total + column_shift(shards[k], plan, depth - k).astype(jnp.float32)
            grads.append(total.astype(jnp.bfloat16))
    home = jnp.stack(
        [jnp.concatenate(grads[0::2], axis=1), jnp.concatenate(grads[1::2], axis=1)]
    )
    home = lax.all_to_all(home, "kvh", split_axis=1, concat_axis=2, tiled=True)
    return (
        jnp.concatenate(attended, axis=1),
        jnp.concatenate(query_grad, axis=1),
        home[0],
        home[1],
    )


def solution(mesh):
    split = P("ctx", "kvh")
    home = P(("ctx", "kvh"), None)
    return jax.shard_map(
        per_device,
        mesh=mesh,
        in_specs=(split, home, home, split, P()),
        out_specs=(split, split, home, home),
        check_vma=False,
    )
```

```python
import functools

import jax
import jax.numpy as jnp
from jax import lax
from jax.experimental import pallas as pl
from jax.experimental.pallas import tpu as pltpu
from jax.sharding import PartitionSpec as P

HD = 128
BLK = 128
GLOB = 2
DEPTH = 4
LOG2E = 1.4426950408889634
NN = (((1,), (0,)), ((), ()))
NT = (((1,), (1,)), ((), ()))
VMEM_LIMIT = 56 * 1024 * 1024
SMALL_VMEM = 16 * 1024 * 1024
COST = pl.CostEstimate(flops=0, bytes_accessed=1 << 10, transcendentals=0)


class Plan:
    def __init__(self, ctx, query_blocks, rand):
        self.ctx, self.qb, self.rand = ctx, query_blocks, rand
        self.sel = 3 + GLOB + rand
        self.depth = DEPTH if ctx % DEPTH == 0 else ctx
        self.lanes = ctx // self.depth
        per_owner = -(-query_blocks * rand // max(1, ctx - 4))
        most, first = 0, []
        for device in range(ctx):
            far = [s for s in range(1, ctx) if abs(s - device) > 1]
            for lane in range(self.lanes):
                there = [s for s in far if s % self.lanes == lane]
                if lane == device % self.lanes:
                    continue
                if device == 0:
                    first.append(there)
                else:
                    most = max(most, len(there))
        over = [there for there in first if len(there) > most]
        self.direct = None
        if len(over) == 1 and len(over[0]) == most + 1:
            self.direct = over[0][0]
        elif over:
            most = max(len(there) for there in over)
        self.slots = 2 + GLOB + min(query_blocks * rand, per_owner * most)
        self.direct_slots = 0 if self.direct is None else min(query_blocks, per_owner)
        self.own = self.depth * query_blocks
        self.far = (self.lanes - 1) * self.slots + self.direct_slots
        self.pool = self.own + self.far

    def column_place(self, me, owner, offset):
        row = lax.rem(me // self.lanes - owner // self.lanes + self.depth, self.depth)
        return row * self.qb + offset

    def place(self, me, owner, offset, slot):
        mine, theirs = lax.rem(me, self.lanes), lax.rem(owner, self.lanes)
        pack = lax.rem(theirs - mine + self.lanes, self.lanes) - 1
        return jnp.where(
            mine == theirs, self.column_place(me, owner, offset), self.own + pack * self.slots + slot
        )


def dot(a, b, dims):
    return lax.dot_general(a, b, dims, preferred_element_type=jnp.float32)


def rows_of(place):
    return pl.ds(pl.multiple_of(place * BLK, BLK), BLK)


def tables_kernel(where, named, table, walk, counts, *, plan):
    qb, rand, lanes = plan.qb, plan.rand, plan.lanes
    sel, named_each = plan.sel, plan.qb * plan.rand
    me = where[0]
    mine = lax.rem(me, lanes)
    left, right = jnp.maximum(me - 1, 0), jnp.minimum(me + 1, plan.ctx - 1)
    for lane in range(lanes):
        counts[lane] = jnp.int32(2 + GLOB)
    counts[lanes] = jnp.int32(0)
    for i in range(qb):
        table[i * sel] = plan.place(me, left, qb - 1, 0) if i == 0 else jnp.int32(i - 1)
        table[i * sel + 1] = jnp.int32(i)
        table[i * sel + 2] = plan.place(me, right, 0, 1) if i == qb - 1 else jnp.int32(i + 1)
        for j in range(GLOB):
            table[i * sel + 3 + j] = plan.place(me, jnp.int32(0), j, 2 + j)
        for j in range(3):
            block = me * qb + i - 1 + j
            counted = (block >= GLOB) & (block < plan.ctx * qb)
            table[qb * sel + i * 3 + j] = counted.astype(jnp.int32)

    def straight(device, owner):
        return jnp.bool_(False) if plan.direct is None else (device == 0) & (owner == plan.direct)

    def entry(n, carry):
        block = named[me * named_each + n]
        owner = block // qb
        apart = straight(me, owner)
        lane = jnp.where(apart, lanes, lax.rem(owner, lanes))
        slot = counts[lane]
        place = plan.place(me, owner, lax.rem(block, qb), slot)
        place = jnp.where(apart, plan.own + (lanes - 1) * plan.slots + slot, place)
        table[(n // rand) * sel + 3 + GLOB + lax.rem(n, rand)] = place
        counts[lane] = slot + 1
        return carry

    lax.fori_loop(0, named_each, entry, 0)

    def clear(n, carry):
        walk[n] = jnp.int32(0)
        return carry

    lax.fori_loop(0, plan.far, clear, 0)
    for step in range(1, lanes):
        base = (step - 1) * plan.slots
        other = me - mine + lax.rem(mine + step, lanes)

        @pl.when((other >= 1) & (lax.rem(other - 1 + lanes, lanes) == mine))
        def _():
            walk[base] = plan.column_place(me, other - 1, qb - 1)

        @pl.when((other + 1 < plan.ctx) & (lax.rem(other + 1, lanes) == mine))
        def _():
            walk[base + 1] = plan.column_place(me, other + 1, 0)

        @pl.when(mine == 0)
        def _():
            for j in range(GLOB):
                walk[base + 2 + j] = plan.column_place(me, jnp.int32(0), j)

        def theirs(n, slot):
            block = named[other * named_each + n]
            owner = block // qb
            hit = (lax.rem(owner, lanes) == mine) & jnp.logical_not(straight(other, owner))

            @pl.when(hit)
            def _():
                walk[base + slot] = plan.column_place(me, owner, lax.rem(block, qb))

            return slot + hit.astype(jnp.int32)

        lax.fori_loop(0, named_each, theirs, jnp.int32(2 + GLOB))
    if plan.direct is not None:

        @pl.when(me == plan.direct)
        def _():
            def zeroth(n, slot):
                block = named[n]
                hit = block // qb == plan.direct

                @pl.when(hit)
                def _():
                    walk[(lanes - 1) * plan.slots + slot] = lax.rem(block, qb)

                return slot + hit.astype(jnp.int32)

            lax.fori_loop(0, named_each, zeroth, jnp.int32(0))


def tables(plan, where, named):
    smem = pl.BlockSpec(memory_space=pltpu.SMEM)
    return pl.pallas_call(
        functools.partial(tables_kernel, plan=plan),
        in_specs=[smem, smem],
        out_specs=[smem, smem],
        out_shape=[
            jax.ShapeDtypeStruct((plan.qb * (plan.sel + 3),), jnp.int32),
            jax.ShapeDtypeStruct((max(1, plan.far),), jnp.int32),
        ],
        scratch_shapes=[pltpu.SMEM((plan.lanes + 1,), jnp.int32)],
        cost_estimate=COST,
        name="list_tables",
    )(where, named)


def whole(a):
    return pl.BlockSpec(a.shape, lambda n, *_: (0, 0))


ANYWHERE = pl.BlockSpec(memory_space=pl.ANY)


def gate_kernel(*refs):
    del refs


def gate(array, *waits):
    return pl.pallas_call(
        gate_kernel,
        in_specs=[ANYWHERE] * (1 + len(waits)),
        out_specs=ANYWHERE,
        out_shape=jax.ShapeDtypeStruct(array.shape, array.dtype),
        input_output_aliases={0: 0},
        cost_estimate=COST,
        name="gate",
    )(array, *waits)


def pack_kernel(walk, *refs, plan, sources, base, slots, size):
    out, pool = refs[-2:]
    rows = plan.qb * BLK
    for t, some in enumerate(sources):
        for k, (n, at) in enumerate(some):
            pool[k * rows : (k + 1) * rows, :] = refs[n][at : at + rows, :]
        for slot in range(slots):
            place = walk[base + slot]
            out[(t * slots + slot) * BLK : (t * slots + slot + 1) * BLK, :] = pool[rows_of(place), :]


def pack(plan, walk, units, step, waits=()):
    rows = plan.qb * BLK
    arrays = [a for unit in units for a in (unit if step else unit[:1])]
    per = plan.depth if step else 1
    halves = units[0][0].shape[0] // rows
    sources = [
        [(u * per + k, half * rows) for k in range(per)] for u in range(len(units)) for half in range(halves)
    ]
    slots = plan.slots if step else plan.direct_slots
    base = (step - 1 if step else plan.lanes - 1) * plan.slots
    size = len(sources) * slots * BLK
    return pl.pallas_call(
        functools.partial(pack_kernel, plan=plan, sources=sources, base=base, slots=slots, size=size),
        grid_spec=pltpu.PrefetchScalarGridSpec(
            num_scalar_prefetch=1,
            grid=(1,),
            in_specs=[whole(a) for a in arrays] + [ANYWHERE] * len(waits),
            out_specs=pl.BlockSpec((size, HD), lambda n, *_: (0, 0)),
            scratch_shapes=[pltpu.VMEM((per * rows, HD), jnp.bfloat16)],
        ),
        out_shape=jax.ShapeDtypeStruct((size, HD), jnp.bfloat16),
        compiler_params=pltpu.CompilerParams(vmem_limit_bytes=SMALL_VMEM),
        cost_estimate=COST,
        name="pack_blocks",
    )(walk, *arrays, *waits)


def merge_kernel(walk, *refs, plan, halves, direct_first):
    rows = plan.qb * BLK
    columns, refs = refs[:halves], refs[halves:]
    packs, refs = refs[: plan.lanes - 1], refs[plan.lanes - 1 :]
    direct = refs[0]
    outs, total = refs[-1 - plan.depth : -1], refs[-1]
    for t in range(halves):
        total[...] = columns[t][...]

        def add(given, slots, first, base):
            for slot in range(slots):
                at = (first + slot) * BLK
                total[rows_of(walk[base + slot]), :] += given[at : at + BLK, :].astype(jnp.float32)

        for step in range(1, plan.lanes):
            add(packs[step - 1], plan.slots, t * plan.slots, (step - 1) * plan.slots)
        if plan.direct is not None:
            add(direct, plan.direct_slots, (direct_first + t) * plan.direct_slots, (plan.lanes - 1) * plan.slots)
        for k in range(plan.depth):
            outs[k][t * rows : (t + 1) * rows, :] = total[k * rows : (k + 1) * rows, :].astype(outs[k].dtype)


def merge(plan, walk, columns, packs, direct, direct_first=0, waits=()):
    halves = len(columns)
    shape = (halves * plan.qb * BLK, HD)
    kinds = [jnp.float32] + [jnp.bfloat16] * (plan.depth - 1)
    args = list(columns) + list(packs) + ([] if direct is None else [direct])
    return pl.pallas_call(
        functools.partial(
            merge_kernel, plan=plan, halves=halves, direct_first=direct_first
        ),
        grid_spec=pltpu.PrefetchScalarGridSpec(
            num_scalar_prefetch=1,
            grid=(1,),
            in_specs=[whole(a) for a in args] + [ANYWHERE] * len(waits),
            out_specs=[pl.BlockSpec(shape, lambda n, *_: (0, 0))] * plan.depth,
            scratch_shapes=[pltpu.VMEM((plan.own * BLK, HD), jnp.float32)],
        ),
        out_shape=[jax.ShapeDtypeStruct(shape, kind) for kind in kinds],
        compiler_params=pltpu.CompilerParams(vmem_limit_bytes=VMEM_LIMIT),
        cost_estimate=COST,
        name="merge_terms",
    )(walk, *args, *waits)


def attend_kernel(table, *refs, plan, qpk, per, given, sources, split):
    q_ref, do_ref = refs[:2]
    parts, refs = refs[2 : 2 + given], refs[2 + given :]
    refs = refs[-(12 + (2 if split else 1) * (plan.lanes - 1) + (plan.direct is not None)) :]
    o_ref, dq_ref, dk_col, dv_col = refs[:4]
    packed, refs = refs[4:-8], refs[-8:]
    kpool, vpool, keys, values, dk_sum, dv_sum, dk_far, dv_far = refs
    i = pl.program_id(0)
    sel = plan.sel
    scale = HD ** -0.5

    @pl.when(i == 0)
    def _():
        for pool, some in zip((kpool, vpool), sources):
            at = 0
            for source, start, size in some:
                pool[at : at + size, :] = parts[source][start : start + size, :]
                at += size
        for total in (dk_col, dv_col, dk_far, dv_far):
            total[...] = jnp.zeros_like(total)

    for j in range(sel):
        place = rows_of(table[i * sel + j])
        keys[j * BLK : (j + 1) * BLK, :] = kpool[place, :]
        values[j * BLK : (j + 1) * BLK, :] = vpool[place, :]
    counted = [table[plan.qb * sel + i * 3 + j] != 0 for j in range(3)]
    K, V = keys[...], values[...]
    KT, VT = K.T, V.T
    for h in range(0, qpk, per):

        def stacked(ref):
            return jnp.concatenate([ref[:, (h + t) * HD : (h + t + 1) * HD] for t in range(per)], axis=0)

        q, do = stacked(q_ref), stacked(do_ref)
        scores = dot(K, q, NT)
        scores = jnp.concatenate(
            [jnp.where(counted[j], scores[j * BLK : (j + 1) * BLK], -jnp.inf) for j in range(3)]
            + [scores[3 * BLK :]],
            axis=0,
        )
        largest = jnp.max(scores, axis=0, keepdims=True)
        raised = jnp.exp2((scores - largest) * (scale * LOG2E))
        inverse = 1.0 / jnp.sum(raised, axis=0, keepdims=True)
        raised_b = raised.astype(jnp.bfloat16)
        attended = dot(VT, raised_b, NN) * inverse
        prob_grad = dot(V, do, NT)
        do_t, q_t = do.T.astype(jnp.float32), q.T.astype(jnp.float32)
        centre = jnp.sum(attended * do_t, axis=0, keepdims=True)
        score_grad = (raised * (prob_grad - centre)).astype(jnp.bfloat16)
        query_grad = dot(KT, score_grad, NN) * (inverse * scale)
        value_grad = dot(raised_b, (do_t * inverse).astype(jnp.bfloat16), NT)
        key_grad = dot(score_grad, (q_t * (inverse * scale)).astype(jnp.bfloat16), NT)
        attended, query_grad = attended.T, query_grad.T
        for t in range(per):
            o_ref[:, (h + t) * HD : (h + t + 1) * HD] = attended[t * BLK : (t + 1) * BLK].astype(jnp.bfloat16)
            dq_ref[:, (h + t) * HD : (h + t + 1) * HD] = query_grad[t * BLK : (t + 1) * BLK].astype(jnp.bfloat16)
        if h == 0:
            dk_sum[...], dv_sum[...] = key_grad, value_grad
        else:
            dk_sum[...] += key_grad
            dv_sum[...] += value_grad
    for j in range(sel):
        place = table[i * sel + j]
        part = slice(j * BLK, (j + 1) * BLK)

        @pl.when(place < plan.own)
        def _():
            dk_col[rows_of(place), :] += dk_sum[part, :]
            dv_col[rows_of(place), :] += dv_sum[part, :]

        @pl.when(place >= plan.own)
        def _():
            dk_far[rows_of(place - plan.own), :] += dk_sum[part, :]
            dv_far[rows_of(place - plan.own), :] += dv_sum[part, :]

    @pl.when(i == plan.qb - 1)
    def _():
        size = plan.slots * BLK
        for t in range(plan.lanes - 1):
            part = slice(t * size, (t + 1) * size)
            if split:
                packed[t][...] = dk_far[part, :].astype(jnp.bfloat16)
                packed[plan.lanes - 1 + t][...] = dv_far[part, :].astype(jnp.bfloat16)
            else:
                packed[t][:size, :] = dk_far[part, :].astype(jnp.bfloat16)
                packed[t][size:, :] = dv_far[part, :].astype(jnp.bfloat16)
        if plan.direct is not None:
            rest = slice((plan.lanes - 1) * size, plan.far * BLK)
            packed[-1][: plan.direct_slots * BLK, :] = dk_far[rest, :].astype(jnp.bfloat16)
            packed[-1][plan.direct_slots * BLK :, :] = dv_far[rest, :].astype(jnp.bfloat16)


def attend(plan, table, queries, out_grad, units, packs, direct, group, qpk, outs, split, waits=()):
    width = qpk * HD
    rows, size = plan.qb * BLK, plan.slots * BLK
    parts, sources = [], [[], []]
    for u, (unit, some) in enumerate(zip(units, packs)):
        for array, step in [(a, rows) for a in unit] + [(a, size) for a in some]:
            for half in range(array.shape[0] // step):
                sources[u + half].append((len(parts), half * step, step))
            parts.append(array)
    if direct is not None:
        step = plan.direct_slots * BLK
        for half in range(2):
            sources[half].append((len(parts), half * step, step))
        parts.append(direct)
    q_spec = pl.BlockSpec((BLK, width), lambda n, *_: (n, group))
    shape = lambda blocks, kind: jax.ShapeDtypeStruct((blocks * BLK, HD), kind)
    o_shape = jax.ShapeDtypeStruct(queries.shape, jnp.bfloat16)
    out_shape = [o_shape, o_shape] + [shape(plan.own, jnp.float32)] * 2
    out_shape += [shape(plan.slots, jnp.bfloat16)] * (2 * (plan.lanes - 1)) if split else [
        shape(2 * plan.slots, jnp.bfloat16)
    ] * (plan.lanes - 1)
    if plan.direct is not None:
        out_shape.append(shape(2 * plan.direct_slots, jnp.bfloat16))
    args = [queries, out_grad, *parts]
    in_specs = [q_spec, q_spec] + [whole(a) for a in args[2:]]
    aliases = {1 + len(args) + t: t for t in range(len(outs))}
    listed = pltpu.VMEM((plan.sel * BLK, HD), jnp.bfloat16)
    listed_sum = pltpu.VMEM((plan.sel * BLK, HD), jnp.float32)
    out = pl.pallas_call(
        functools.partial(
            attend_kernel, plan=plan, qpk=qpk, per=4 if qpk % 4 == 0 else 1, given=len(parts), sources=sources, split=split
        ),
        grid_spec=pltpu.PrefetchScalarGridSpec(
            num_scalar_prefetch=1,
            grid=(plan.qb,),
            in_specs=in_specs + [ANYWHERE] * (len(outs) + len(waits)),
            out_specs=[q_spec, q_spec] + [whole(s) for s in out_shape[2:]],
            scratch_shapes=[pltpu.VMEM((plan.pool * BLK, HD), jnp.bfloat16)] * 2
            + [listed, listed, listed_sum, listed_sum]
            + [pltpu.VMEM((plan.far * BLK, HD), jnp.float32)] * 2,
        ),
        out_shape=out_shape,
        input_output_aliases=aliases,
        compiler_params=pltpu.CompilerParams(vmem_limit_bytes=VMEM_LIMIT),
        cost_estimate=COST,
        name="attend_head",
    )(table, *args, *outs, *waits)
    outs, columns, far = out[:2], out[2:4], list(out[4:])
    straight = far.pop() if plan.direct is not None else None
    return outs, columns, ([far[: plan.lanes - 1], far[plan.lanes - 1 :]] if split else [far], straight)


def column_shift(array, plan, rows):
    return lax.ppermute(array, "ctx", [(n, (n + rows * plan.lanes) % plan.ctx) for n in range(plan.ctx)])


def row_shift(array, plan, lanes):
    return lax.ppermute(
        array, "ctx", [(n, n - n % plan.lanes + (n + lanes) % plan.lanes) for n in range(plan.ctx)]
    )


def straight_shift(array, plan, there, back):
    return lax.ppermute(array, "ctx", [(there, back)])


def to_heads(arrays, group, groups):
    size = lax.axis_size("kvh")
    parts = jnp.stack([a.reshape(a.shape[0], size, groups, HD)[:, :, group] for a in arrays])
    parts = lax.all_to_all(parts.transpose(2, 0, 1, 3), "kvh", split_axis=0, concat_axis=0, tiled=True)
    return jnp.moveaxis(parts, 1, 0).reshape(-1, HD)


def to_tokens(array, count):
    size = lax.axis_size("kvh")
    parts = jnp.moveaxis(array.reshape(count, size, -1, HD), 1, 0)
    parts = lax.all_to_all(parts, "kvh", split_axis=0, concat_axis=0, tiled=True)
    return [parts[:, t] for t in range(count)]


def per_device(queries, keys, values, out_grad, random_blocks):
    kvh = lax.axis_size("kvh")
    groups = keys.shape[1] // (kvh * HD)
    qpk = queries.shape[1] // (groups * HD)
    plan = Plan(lax.axis_size("ctx"), queries.shape[0] // BLK, random_blocks.shape[1])
    lanes, depth, qb = plan.lanes, plan.depth, plan.qb
    where = lax.axis_index("ctx").astype(jnp.int32).reshape(1)
    table, walk = tables(plan, where, random_blocks.reshape(-1))

    def spread(own):
        return [own] + [column_shift(own, plan, k) for k in range(1, depth)]

    def across(units, waits=()):
        return [row_shift(pack(plan, walk, units, lanes - t, waits), plan, lanes - t) for t in range(1, lanes)]

    def straight(units, waits=()):
        if plan.direct is None:
            return None
        return straight_shift(pack(plan, walk, units, 0, waits), plan, plan.direct, 0)

    def send_back(packs):
        return [row_shift(packs[t - 1], plan, t) for t in range(1, lanes)][::-1]

    def home(terms, count):
        arrived = [column_shift(terms[k], plan, depth - k) for k in range(1, depth)]
        total = terms[0]
        for array in arrived:
            total = total + array.astype(jnp.float32)
        return to_tokens(total.astype(jnp.bfloat16), count), arrived

    own = [to_heads([a], 0, groups) for a in (keys, values)]
    units = [spread(a) for a in own]
    direct = straight([[a] for a in own], tuple(units[0][1:]))
    packs = [across([unit]) for unit in units]
    homes, outs, waits, arrived = [], [], (), []
    for g in range(groups):
        last = g + 1 == groups
        if not last:
            ready = [a for unit in units for a in unit[1:]]
            coming = gate(to_heads([keys, values], g + 1, groups), *ready)
            coming_units = [spread(coming)]
            coming_direct = straight([[coming]])
        outs, columns, (far, far_direct) = attend(
            plan, table, queries, out_grad, units, packs, direct, g, qpk, outs, last, waits
        )
        if far_direct is not None:
            far_direct = straight_shift(far_direct, plan, 0, plan.direct)
        if not last:
            far = [[gate(a, *coming_units[0][1:]) for a in far[0]]]
        backs = [send_back(some) for some in far]
        if last:
            for t in range(2):
                terms = merge(plan, walk, [columns[t]], backs[t], far_direct, direct_first=t, waits=tuple(arrived))
                homes.append(home(terms, 1)[0])
        else:
            terms = merge(plan, walk, columns, backs[0], far_direct, waits=tuple(arrived))
            total, arrived = home(terms, 2)
            homes.append(total)
            waits = (terms[1],)
            units, direct = coming_units, coming_direct
            packs = [across(units, tuple(backs[0]))]
    homes[-2:] = [homes[-2] + homes[-1]]
    key_grad, value_grad = (
        jnp.stack([some[n] for some in homes], axis=2).transpose(1, 0, 2, 3).reshape(keys.shape) for n in range(2)
    )
    return outs[0], outs[1], key_grad, value_grad


def solution(mesh):
    split = P("ctx", "kvh")
    home = P(("ctx", "kvh"), None)
    return jax.shard_map(
        per_device,
        mesh=mesh,
        in_specs=(split, home, home, split, P()),
        out_specs=(split, split, home, home),
        check_vma=False,
    )
```

```python
import functools

import jax
import jax.numpy as jnp
from jax import lax
from jax.experimental import pallas as pl
from jax.experimental.pallas import tpu as pltpu
from jax.sharding import PartitionSpec as P

HD = 128
BLK = 128
GLOB = 2
DEPTH = 4
LOG2E = 1.4426950408889634
NN = (((1,), (0,)), ((), ()))
NT = (((1,), (1,)), ((), ()))
VMEM_LIMIT = 56 * 1024 * 1024
SMALL_VMEM = 16 * 1024 * 1024
COST = pl.CostEstimate(flops=0, bytes_accessed=1 << 10, transcendentals=0)


class Plan:
    def __init__(self, ctx, query_blocks, rand):
        self.ctx, self.qb, self.rand = ctx, query_blocks, rand
        self.sel = 3 + GLOB + rand
        self.depth = DEPTH if ctx % DEPTH == 0 else ctx
        self.lanes = ctx // self.depth
        per_owner = -(-query_blocks * rand // max(1, ctx - 4))
        most, first = 0, []
        for device in range(ctx):
            far = [s for s in range(1, ctx) if abs(s - device) > 1]
            for lane in range(self.lanes):
                there = [s for s in far if s % self.lanes == lane]
                if lane == device % self.lanes:
                    continue
                if device == 0:
                    first.append(there)
                else:
                    most = max(most, len(there))
        over = [there for there in first if len(there) > most]
        self.direct = None
        if len(over) == 1 and len(over[0]) == most + 1:
            self.direct = over[0][0]
        elif over:
            most = max(len(there) for there in over)
        self.slots = 2 + GLOB + min(query_blocks * rand, per_owner * most)
        self.direct_slots = 0 if self.direct is None else min(query_blocks, per_owner)
        self.row_slots = {}
        for step in range(1, self.depth):
            most_here = 0
            for device in range(ctx):
                row = (device // self.lanes - step) % self.depth
                inside = [s for s in range(ctx) if s // self.lanes == row]
                size = GLOB * (row == 0) + sum(abs(s - device) == 1 for s in inside)
                size += min(query_blocks * rand, per_owner * sum(s > 0 and abs(s - device) > 1 for s in inside))
                most_here = max(most_here, size)
            self.row_slots[step] = most_here
        self.own = self.depth * query_blocks
        self.far = (self.lanes - 1) * self.slots + self.direct_slots
        self.pool = self.own + self.far

    def column_place(self, me, owner, offset):
        row = lax.rem(me // self.lanes - owner // self.lanes + self.depth, self.depth)
        return row * self.qb + offset

    def place(self, me, owner, offset, slot):
        mine, theirs = lax.rem(me, self.lanes), lax.rem(owner, self.lanes)
        pack = lax.rem(theirs - mine + self.lanes, self.lanes) - 1
        return jnp.where(
            mine == theirs, self.column_place(me, owner, offset), self.own + pack * self.slots + slot
        )


def dot(a, b, dims):
    return lax.dot_general(a, b, dims, preferred_element_type=jnp.float32)


def rows_of(place):
    return pl.ds(pl.multiple_of(place * BLK, BLK), BLK)


def tables_kernel(where, named, table, walk, counts, *, plan):
    qb, rand, lanes = plan.qb, plan.rand, plan.lanes
    sel, named_each = plan.sel, plan.qb * plan.rand
    me = where[0]
    mine = lax.rem(me, lanes)
    left, right = jnp.maximum(me - 1, 0), jnp.minimum(me + 1, plan.ctx - 1)
    for lane in range(lanes):
        counts[lane] = jnp.int32(2 + GLOB)
    counts[lanes] = jnp.int32(0)
    for i in range(qb):
        table[i * sel] = plan.place(me, left, qb - 1, 0) if i == 0 else jnp.int32(i - 1)
        table[i * sel + 1] = jnp.int32(i)
        table[i * sel + 2] = plan.place(me, right, 0, 1) if i == qb - 1 else jnp.int32(i + 1)
        for j in range(GLOB):
            table[i * sel + 3 + j] = plan.place(me, jnp.int32(0), j, 2 + j)
        for j in range(3):
            block = me * qb + i - 1 + j
            counted = (block >= GLOB) & (block < plan.ctx * qb)
            table[qb * sel + i * 3 + j] = counted.astype(jnp.int32)

    def straight(device, owner):
        return jnp.bool_(False) if plan.direct is None else (device == 0) & (owner == plan.direct)

    def entry(n, carry):
        block = named[me * named_each + n]
        owner = block // qb
        apart = straight(me, owner)
        lane = jnp.where(apart, lanes, lax.rem(owner, lanes))
        slot = counts[lane]
        place = plan.place(me, owner, lax.rem(block, qb), slot)
        place = jnp.where(apart, plan.own + (lanes - 1) * plan.slots + slot, place)
        table[(n // rand) * sel + 3 + GLOB + lax.rem(n, rand)] = place
        counts[lane] = slot + 1
        return carry

    lax.fori_loop(0, named_each, entry, 0)

    def clear(n, carry):
        walk[n] = jnp.int32(0)
        return carry

    lax.fori_loop(0, plan.far, clear, 0)
    for step in range(1, lanes):
        base = (step - 1) * plan.slots
        other = me - mine + lax.rem(mine + step, lanes)

        @pl.when((other >= 1) & (lax.rem(other - 1 + lanes, lanes) == mine))
        def _():
            walk[base] = plan.column_place(me, other - 1, qb - 1)

        @pl.when((other + 1 < plan.ctx) & (lax.rem(other + 1, lanes) == mine))
        def _():
            walk[base + 1] = plan.column_place(me, other + 1, 0)

        @pl.when(mine == 0)
        def _():
            for j in range(GLOB):
                walk[base + 2 + j] = plan.column_place(me, jnp.int32(0), j)

        def theirs(n, slot):
            block = named[other * named_each + n]
            owner = block // qb
            hit = (lax.rem(owner, lanes) == mine) & jnp.logical_not(straight(other, owner))

            @pl.when(hit)
            def _():
                walk[base + slot] = plan.column_place(me, owner, lax.rem(block, qb))

            return slot + hit.astype(jnp.int32)

        lax.fori_loop(0, named_each, theirs, jnp.int32(2 + GLOB))
    if plan.direct is not None:

        @pl.when(me == plan.direct)
        def _():
            def zeroth(n, slot):
                block = named[n]
                hit = block // qb == plan.direct

                @pl.when(hit)
                def _():
                    walk[(lanes - 1) * plan.slots + slot] = lax.rem(block, qb)

                return slot + hit.astype(jnp.int32)

            lax.fori_loop(0, named_each, zeroth, jnp.int32(0))


def tables(plan, where, named):
    smem = pl.BlockSpec(memory_space=pltpu.SMEM)
    return pl.pallas_call(
        functools.partial(tables_kernel, plan=plan),
        in_specs=[smem, smem],
        out_specs=[smem, smem],
        out_shape=[
            jax.ShapeDtypeStruct((plan.qb * (plan.sel + 3),), jnp.int32),
            jax.ShapeDtypeStruct((max(1, plan.far),), jnp.int32),
        ],
        scratch_shapes=[pltpu.SMEM((plan.lanes + 1,), jnp.int32)],
        cost_estimate=COST,
        name="list_tables",
    )(where, named)


def row_tables_kernel(where, named, table, walk, counts, *, plan):
    qb, rand, lanes, depth, ctx = plan.qb, plan.rand, plan.lanes, plan.depth, plan.ctx
    sel, named_each = plan.sel, plan.qb * plan.rand
    me = where[0]
    mine, row = lax.rem(me, lanes), me // lanes

    def in_row(owner, offset):
        return lax.rem(lax.rem(owner, lanes) - mine + lanes, lanes) * qb + offset

    def walk_list(device, there, visit):
        for j in range(GLOB):
            pl.when(there == 0)(functools.partial(visit, jnp.int32(0), j, 3 + j))
        pl.when((device >= 1) & ((device - 1) // lanes == there))(functools.partial(visit, device - 1, qb - 1, 0))
        right = (device + 1 < ctx) & ((device + 1) // lanes == there)
        pl.when(right)(functools.partial(visit, device + 1, 0, (qb - 1) * sel + 2))

        def entry(n, carry):
            block = named[device * named_each + n]
            owner = block // qb
            at = (n // rand) * sel + 3 + GLOB + lax.rem(n, rand)
            pl.when(owner // lanes == there)(functools.partial(visit, owner, lax.rem(block, qb), at))
            return carry

        lax.fori_loop(0, named_each, entry, 0)

    for i in range(qb):
        table[i * sel] = jnp.int32(max(i - 1, 0))
        table[i * sel + 1] = jnp.int32(i)
        table[i * sel + 2] = jnp.int32(min(i + 1, qb - 1))

    def beside(owner, offset, at):
        table[at] = in_row(owner, offset)

    walk_list(me, row, beside)
    base, begin = lanes * qb, 0
    for step, slots in plan.row_slots.items():
        counts[0] = jnp.int32(0)

        def found(owner, offset, at, base=base):
            table[at] = base + counts[0]
            counts[0] = counts[0] + 1

        walk_list(me, lax.rem(row - step + depth, depth), found)
        counts[0] = jnp.int32(0)
        for n in range(slots):
            walk[begin + n] = jnp.int32(0)

        def asked(owner, offset, at, begin=begin):
            walk[begin + counts[0]] = in_row(owner, offset)
            counts[0] = counts[0] + 1

        walk_list(lax.rem(row + step, depth) * lanes + mine, row, asked)
        base, begin = base + slots, begin + slots
    for i in range(1, qb):
        for j in range(GLOB):
            table[i * sel + 3 + j] = table[3 + j]


def row_tables(plan, where, named):
    smem = pl.BlockSpec(memory_space=pltpu.SMEM)
    return pl.pallas_call(
        functools.partial(row_tables_kernel, plan=plan),
        in_specs=[smem, smem],
        out_specs=[smem, smem],
        out_shape=[
            jax.ShapeDtypeStruct((plan.qb * plan.sel,), jnp.int32),
            jax.ShapeDtypeStruct((sum(plan.row_slots.values()),), jnp.int32),
        ],
        scratch_shapes=[pltpu.SMEM((1,), jnp.int32)],
        cost_estimate=COST,
        name="row_tables",
    )(where, named)


def pack_rows_kernel(walk, *refs, plan):
    shards, outs, pool = refs[: plan.lanes], refs[-plan.depth : -1], refs[-1]
    rows = plan.qb * BLK
    for t in range(2):
        for lane, shard in enumerate(shards):
            pool[lane * rows : (lane + 1) * rows, :] = shard[t * rows : (t + 1) * rows, :]
        begin = 0
        for out, slots in zip(outs, plan.row_slots.values()):
            for slot in range(slots):
                place = rows_of(walk[begin + slot])
                out[(t * slots + slot) * BLK : (t * slots + slot + 1) * BLK, :] = pool[place, :]
            begin += slots


def pack_rows(plan, walk, shards, waits):
    shapes = [jax.ShapeDtypeStruct((2 * slots * BLK, HD), jnp.bfloat16) for slots in plan.row_slots.values()]
    return pl.pallas_call(
        functools.partial(pack_rows_kernel, plan=plan),
        grid_spec=pltpu.PrefetchScalarGridSpec(
            num_scalar_prefetch=1,
            grid=(1,),
            in_specs=[whole(a) for a in shards] + [ANYWHERE] * len(waits),
            out_specs=[whole(s) for s in shapes],
            scratch_shapes=[pltpu.VMEM((plan.lanes * plan.qb * BLK, HD), jnp.bfloat16)],
        ),
        out_shape=shapes,
        compiler_params=pltpu.CompilerParams(vmem_limit_bytes=SMALL_VMEM),
        cost_estimate=COST,
        name="pack_rows",
    )(walk, *shards, *waits)


def whole(a):
    return pl.BlockSpec(a.shape, lambda n, *_: (0, 0))


ANYWHERE = pl.BlockSpec(memory_space=pl.ANY)


def gate_kernel(*refs):
    del refs


def gate(array, *waits):
    return pl.pallas_call(
        gate_kernel,
        in_specs=[ANYWHERE] * (1 + len(waits)),
        out_specs=ANYWHERE,
        out_shape=jax.ShapeDtypeStruct(array.shape, array.dtype),
        input_output_aliases={0: 0},
        cost_estimate=COST,
        name="gate",
    )(array, *waits)


def pack_kernel(walk, *refs, plan, sources, base, slots, size):
    out, pool = refs[-2:]
    rows = plan.qb * BLK
    for t, some in enumerate(sources):
        for k, (n, at) in enumerate(some):
            pool[k * rows : (k + 1) * rows, :] = refs[n][at : at + rows, :]
        for slot in range(slots):
            place = walk[base + slot]
            out[(t * slots + slot) * BLK : (t * slots + slot + 1) * BLK, :] = pool[rows_of(place), :]


def pack(plan, walk, units, step, waits=()):
    rows = plan.qb * BLK
    arrays = [a for unit in units for a in (unit if step else unit[:1])]
    per = plan.depth if step else 1
    halves = units[0][0].shape[0] // rows
    sources = [
        [(u * per + k, half * rows) for k in range(per)] for u in range(len(units)) for half in range(halves)
    ]
    slots = plan.slots if step else plan.direct_slots
    base = (step - 1 if step else plan.lanes - 1) * plan.slots
    size = len(sources) * slots * BLK
    return pl.pallas_call(
        functools.partial(pack_kernel, plan=plan, sources=sources, base=base, slots=slots, size=size),
        grid_spec=pltpu.PrefetchScalarGridSpec(
            num_scalar_prefetch=1,
            grid=(1,),
            in_specs=[whole(a) for a in arrays] + [ANYWHERE] * len(waits),
            out_specs=pl.BlockSpec((size, HD), lambda n, *_: (0, 0)),
            scratch_shapes=[pltpu.VMEM((per * rows, HD), jnp.bfloat16)],
        ),
        out_shape=jax.ShapeDtypeStruct((size, HD), jnp.bfloat16),
        compiler_params=pltpu.CompilerParams(vmem_limit_bytes=SMALL_VMEM),
        cost_estimate=COST,
        name="pack_blocks",
    )(walk, *arrays, *waits)


def merge_kernel(walk, *refs, plan, halves, direct_first):
    rows = plan.qb * BLK
    columns, refs = refs[:halves], refs[halves:]
    packs, refs = refs[: halves * (plan.lanes - 1)], refs[halves * (plan.lanes - 1) :]
    direct = refs[0]
    outs, total = refs[-1 - plan.depth : -1], refs[-1]
    for t in range(halves):
        total[...] = columns[t][...]

        def add(given, slots, first, base):
            for slot in range(slots):
                at = (first + slot) * BLK
                total[rows_of(walk[base + slot]), :] += given[at : at + BLK, :].astype(jnp.float32)

        for step in range(1, plan.lanes):
            add(packs[t * (plan.lanes - 1) + step - 1], plan.slots, 0, (step - 1) * plan.slots)
        if plan.direct is not None:
            add(direct, plan.direct_slots, (direct_first + t) * plan.direct_slots, (plan.lanes - 1) * plan.slots)
        for k in range(plan.depth):
            outs[k][t * rows : (t + 1) * rows, :] = total[k * rows : (k + 1) * rows, :].astype(outs[k].dtype)


def merge(plan, walk, columns, packs, direct, direct_first=0, waits=()):
    halves = len(columns)
    shape = (halves * plan.qb * BLK, HD)
    kinds = [jnp.float32] + [jnp.bfloat16] * (plan.depth - 1)
    args = list(columns) + [a for some in packs for a in some] + ([] if direct is None else [direct])
    return pl.pallas_call(
        functools.partial(
            merge_kernel, plan=plan, halves=halves, direct_first=direct_first
        ),
        grid_spec=pltpu.PrefetchScalarGridSpec(
            num_scalar_prefetch=1,
            grid=(1,),
            in_specs=[whole(a) for a in args] + [ANYWHERE] * len(waits),
            out_specs=[pl.BlockSpec(shape, lambda n, *_: (0, 0))] * plan.depth,
            scratch_shapes=[pltpu.VMEM((plan.own * BLK, HD), jnp.float32)],
        ),
        out_shape=[jax.ShapeDtypeStruct(shape, kind) for kind in kinds],
        compiler_params=pltpu.CompilerParams(vmem_limit_bytes=VMEM_LIMIT),
        cost_estimate=COST,
        name="merge_terms",
    )(walk, *args, *waits)


def attend_kernel(found, table, *refs, plan, qpk, per, given, sources, split, first, ends):
    q_ref, do_ref = refs[:2]
    parts, refs = refs[2 : 2 + given], refs[2 + given :]
    before = refs[: 2 if first else 0]
    if ends:
        refs = refs[-(12 + (2 if split else 1) * (plan.lanes - 1) + (plan.direct is not None)) :]
        o_ref, dq_ref, dk_col, dv_col = refs[:4]
        packed, refs = refs[4:-8], refs[-8:]
        kpool, vpool, keys, values, dk_sum, dv_sum, dk_far, dv_far = refs
    else:
        o_ref, dq_ref, dk_sum, dv_sum, kpool, vpool, keys, values = refs[-8:]
    n = pl.program_id(0)
    i = n + first
    sel = plan.sel
    scale = HD ** -0.5

    def add(i, k_terms, v_terms, base):
        for j in range(sel):
            place = table[i * sel + j]
            part = slice(base + j * BLK, base + (j + 1) * BLK)

            @pl.when(place < plan.own)
            def _():
                dk_col[rows_of(place), :] += k_terms[part, :]
                dv_col[rows_of(place), :] += v_terms[part, :]

            @pl.when(place >= plan.own)
            def _():
                dk_far[rows_of(place - plan.own), :] += k_terms[part, :]
                dv_far[rows_of(place - plan.own), :] += v_terms[part, :]

    @pl.when(n == 0)
    def _():
        for pool, some in zip((kpool, vpool), sources):
            at = 0
            for source, start, size in some:
                pool[at : at + size, :] = parts[source][start : start + size, :]
                at += size
        if ends:
            for total in (dk_col, dv_col, dk_far, dv_far):
                total[...] = jnp.zeros_like(total)
        for done in range(first):
            add(done, *before, done * sel * BLK)

    for j in range(sel):
        place = rows_of(found[i * sel + j])
        keys[j * BLK : (j + 1) * BLK, :] = kpool[place, :]
        values[j * BLK : (j + 1) * BLK, :] = vpool[place, :]
    counted = [table[plan.qb * sel + i * 3 + j] != 0 for j in range(3)]
    K, V = keys[...], values[...]
    KT, VT = K.T, V.T
    for h in range(0, qpk, per):

        def stacked(ref):
            return jnp.concatenate([ref[:, (h + t) * HD : (h + t + 1) * HD] for t in range(per)], axis=0)

        q, do = stacked(q_ref), stacked(do_ref)
        scores = dot(K, q, NT)
        scores = jnp.concatenate(
            [jnp.where(counted[j], scores[j * BLK : (j + 1) * BLK], -jnp.inf) for j in range(3)]
            + [scores[3 * BLK :]],
            axis=0,
        )
        largest = jnp.max(scores, axis=0, keepdims=True)
        raised = jnp.exp2((scores - largest) * (scale * LOG2E))
        inverse = 1.0 / jnp.sum(raised, axis=0, keepdims=True)
        raised_b = raised.astype(jnp.bfloat16)
        attended = dot(VT, raised_b, NN) * inverse
        prob_grad = dot(V, do, NT)
        do_t, q_t = do.T.astype(jnp.float32), q.T.astype(jnp.float32)
        centre = jnp.sum(attended * do_t, axis=0, keepdims=True)
        score_grad = (raised * (prob_grad - centre)).astype(jnp.bfloat16)
        query_grad = dot(KT, score_grad, NN) * (inverse * scale)
        value_grad = dot(raised_b, (do_t * inverse).astype(jnp.bfloat16), NT)
        key_grad = dot(score_grad, (q_t * (inverse * scale)).astype(jnp.bfloat16), NT)
        attended, query_grad = attended.T, query_grad.T
        for t in range(per):
            o_ref[:, (h + t) * HD : (h + t + 1) * HD] = attended[t * BLK : (t + 1) * BLK].astype(jnp.bfloat16)
            dq_ref[:, (h + t) * HD : (h + t + 1) * HD] = query_grad[t * BLK : (t + 1) * BLK].astype(jnp.bfloat16)
        if h == 0:
            dk_sum[...], dv_sum[...] = key_grad, value_grad
        else:
            dk_sum[...] += key_grad
            dv_sum[...] += value_grad
    if not ends:
        return
    add(i, dk_sum, dv_sum, 0)

    @pl.when(i == plan.qb - 1)
    def _():
        size = plan.slots * BLK
        for t in range(plan.lanes - 1):
            part = slice(t * size, (t + 1) * size)
            if split:
                packed[t][...] = dk_far[part, :].astype(jnp.bfloat16)
                packed[plan.lanes - 1 + t][...] = dv_far[part, :].astype(jnp.bfloat16)
            else:
                packed[t][:size, :] = dk_far[part, :].astype(jnp.bfloat16)
                packed[t][size:, :] = dv_far[part, :].astype(jnp.bfloat16)
        if plan.direct is not None:
            rest = slice((plan.lanes - 1) * size, plan.far * BLK)
            packed[-1][: plan.direct_slots * BLK, :] = dk_far[rest, :].astype(jnp.bfloat16)
            packed[-1][plan.direct_slots * BLK :, :] = dv_far[rest, :].astype(jnp.bfloat16)


def attend(plan, found, table, queries, out_grad, pieces, group, qpk, outs, split, first, count, terms=(), waits=()):
    width = qpk * HD
    parts, sources = [], [[], []]
    for array, kind, step in pieces:
        for half in range(2):
            if kind == half:
                sources[half].append((len(parts), 0, step))
            elif kind == 2:
                sources[half] += [(len(parts), at + half * step, step) for at in range(0, array.shape[0], 2 * step)]
        parts.append(array)
    pool = pltpu.VMEM((sum(step for _, _, step in sources[0]), HD), jnp.bfloat16)
    q_spec = pl.BlockSpec((BLK, width), lambda n, *_: (n + first, group))
    shape = lambda blocks, kind: jax.ShapeDtypeStruct((blocks * BLK, HD), kind)
    o_shape = jax.ShapeDtypeStruct(queries.shape, jnp.bfloat16)
    ends = first + count == plan.qb
    out_shape = [o_shape, o_shape] + [shape(plan.own if ends else count * plan.sel, jnp.float32)] * 2
    if ends:
        out_shape += [shape((1 if split else 2) * plan.slots, jnp.bfloat16)] * ((2 if split else 1) * (plan.lanes - 1))
    if ends and plan.direct is not None:
        out_shape.append(shape(2 * plan.direct_slots, jnp.bfloat16))
    args = [queries, out_grad, *parts, *terms]
    in_specs = [q_spec, q_spec] + [whole(a) for a in args[2:]]
    aliases = {2 + len(args) + t: t for t in range(len(outs))}
    listed = pltpu.VMEM((plan.sel * BLK, HD), jnp.bfloat16)
    term_spec = pl.BlockSpec((plan.sel * BLK, HD), lambda n, *_: (n, 0))
    listed_sum = pltpu.VMEM((plan.sel * BLK, HD), jnp.float32)
    out = pl.pallas_call(
        functools.partial(
            attend_kernel, plan=plan, qpk=qpk, per=4 if qpk % 4 == 0 else 1, given=len(parts), sources=sources, split=split,
            first=first, ends=ends,
        ),
        grid_spec=pltpu.PrefetchScalarGridSpec(
            num_scalar_prefetch=2,
            grid=(count,),
            in_specs=in_specs + [ANYWHERE] * (len(outs) + len(waits)),
            out_specs=[q_spec, q_spec] + ([whole(s) for s in out_shape[2:]] if ends else [term_spec] * 2),
            scratch_shapes=[pool] * 2
            + [listed, listed]
            + ([listed_sum, listed_sum] + [pltpu.VMEM((plan.far * BLK, HD), jnp.float32)] * 2 if ends else []),
        ),
        out_shape=out_shape,
        input_output_aliases=aliases,
        compiler_params=pltpu.CompilerParams(vmem_limit_bytes=VMEM_LIMIT),
        cost_estimate=COST,
        name="attend_head",
    )(found, table, *args, *outs, *waits)
    outs, columns, far = out[:2], out[2:4], list(out[4:])
    if not ends:
        return outs, columns, None
    straight = far.pop() if plan.direct is not None else None
    return outs, columns, ([far[: plan.lanes - 1], far[plan.lanes - 1 :]] if split else [far], straight)


def column_shift(array, plan, rows):
    return lax.ppermute(array, "ctx", [(n, (n + rows * plan.lanes) % plan.ctx) for n in range(plan.ctx)])


def row_shift(array, plan, lanes):
    return lax.ppermute(
        array, "ctx", [(n, n - n % plan.lanes + (n + lanes) % plan.lanes) for n in range(plan.ctx)]
    )


def straight_shift(array, plan, there, back):
    return lax.ppermute(array, "ctx", [(there, back)])


def cut_kernel(keys, values, out, *, size, groups):
    for n in range(size):
        for g in range(groups):
            part = slice((n * groups + g) * HD, (n * groups + g + 1) * HD)
            out[n, 2 * g] = keys[:, part]
            out[n, 2 * g + 1] = values[:, part]


def join_kernel(parts, *outs, size, groups):
    rows = parts.shape[2]
    for n in range(size):
        for g in range(groups):
            for t in range(2):
                out, at = (outs[t], 0) if g == 0 else (outs[1 + g], t * size * rows)
                out[at + n * rows : at + (n + 1) * rows, :] = parts[n, 2 * g + t]


def to_heads(keys, values, groups):
    size = lax.axis_size("kvh")
    rows = keys.shape[0]
    vmem = pl.BlockSpec(memory_space=pltpu.VMEM)
    parts = pl.pallas_call(
        functools.partial(cut_kernel, size=size, groups=groups),
        in_specs=[vmem, vmem],
        out_specs=vmem,
        out_shape=jax.ShapeDtypeStruct((size, 2 * groups, rows, HD), keys.dtype),
        cost_estimate=COST,
        name="cut_heads",
    )(keys, values)
    parts = lax.all_to_all(parts, "kvh", split_axis=0, concat_axis=0, tiled=True)
    shapes = [(size * rows, HD)] * 2 + [(2 * size * rows, HD)] * (groups - 1)
    return pl.pallas_call(
        functools.partial(join_kernel, size=size, groups=groups),
        in_specs=[vmem],
        out_specs=[vmem] * len(shapes),
        out_shape=[jax.ShapeDtypeStruct(shape, keys.dtype) for shape in shapes],
        cost_estimate=COST,
        name="join_heads",
    )(parts)


def to_tokens(array, count):
    size = lax.axis_size("kvh")
    parts = jnp.moveaxis(array.reshape(count, size, -1, HD), 1, 0)
    parts = lax.all_to_all(parts, "kvh", split_axis=0, concat_axis=0, tiled=True)
    return [parts[:, t] for t in range(count)]


def per_device(queries, keys, values, out_grad, random_blocks):
    kvh = lax.axis_size("kvh")
    groups = keys.shape[1] // (kvh * HD)
    qpk = queries.shape[1] // (groups * HD)
    plan = Plan(lax.axis_size("ctx"), queries.shape[0] // BLK, random_blocks.shape[1])
    lanes, depth, qb = plan.lanes, plan.depth, plan.qb
    where = lax.axis_index("ctx").astype(jnp.int32).reshape(1)
    table, walk = tables(plan, where, random_blocks.reshape(-1))

    def spread(own):
        return [own] + [column_shift(own, plan, k) for k in range(1, depth)]

    def across(units, waits=()):
        return [row_shift(pack(plan, walk, units, lanes - t, waits), plan, lanes - t) for t in range(1, lanes)]

    def straight(units, waits=()):
        if plan.direct is None:
            return None
        return straight_shift(pack(plan, walk, units, 0, waits), plan, plan.direct, 0)

    def send_back(packs):
        return [row_shift(packs[t - 1], plan, t) for t in range(1, lanes)][::-1]

    def home(terms, count):
        arrived = [column_shift(terms[k], plan, depth - k) for k in range(1, depth)]
        total = terms[0]
        for array in arrived:
            total = total + array.astype(jnp.float32)
        return to_tokens(total.astype(jnp.bfloat16), count), arrived

    rows, size = qb * BLK, plan.slots * BLK
    own = to_heads(keys, values, groups)
    own, joined = own[:2], own[2:]
    units = [spread(a) for a in own]
    direct = straight([[a] for a in own], tuple(units[0][1:]))
    in_row = [[a] + [row_shift(a, plan, lanes - t) for t in range(1, lanes)] for a in joined]
    packs = [across([units[0]], tuple(a for some in in_row for a in some[1:]))]
    packs.append(across([units[1]], (*packs[0], *([] if direct is None else [direct]))))
    pieces = [(a, t, rows) for t in range(2) for a in units[t]] + [(a, t, size) for t in range(2) for a in packs[t]]
    if direct is not None:
        pieces.append((direct, 2, plan.direct_slots * BLK))
    ready = [a for unit in units for a in unit[1:]]
    found, homes, outs, arrived, waits = table, [], [], [], ()
    if groups > 1:
        row_found, row_walk = row_tables(plan, where, random_blocks.reshape(-1))
    for g in range(groups):
        last = g + 1 == groups
        if not last:
            sent = pack_rows(plan, row_walk, in_row[g], tuple(ready))
            waits = (sent[0],)
            ready = [column_shift(a, plan, step) for a, step in zip(sent, plan.row_slots)]
        run = functools.partial(attend, plan, found, table, queries, out_grad, pieces, g, qpk)
        if not g:
            outs, columns, (far, far_direct) = run(outs, True, 0, qb, (), waits)
        else:
            before = merge(plan, walk, *before, waits=tuple(a for a, _, _ in pieces))
            total, arrived = home(before, 2)
            homes.append(total)
            outs, columns, (far, far_direct) = run(outs, True, 0, qb, (), (before[1],))
        if arrived:
            far[1] = [gate(a, *arrived) for a in far[1]]
            far_direct = far_direct if far_direct is None else gate(far_direct, *arrived)
        if far_direct is not None:
            far_direct = straight_shift(far_direct, plan, 0, plan.direct)
        backs = [send_back(some) for some in far]
        if last:
            for t in range(2):
                terms = merge(plan, walk, [columns[t]], [backs[t]], far_direct, direct_first=t)
                homes.append(home(terms, 1)[0])
        else:
            before = columns, backs, far_direct
            found, pieces = row_found, [(a, 2, rows) for a in in_row[g]]
            pieces += [(a, 2, slots * BLK) for a, slots in zip(ready, plan.row_slots.values())]
    homes[-2:] = [homes[-2] + homes[-1]]
    key_grad, value_grad = (
        jnp.stack([some[n] for some in homes], axis=2).transpose(1, 0, 2, 3).reshape(keys.shape) for n in range(2)
    )
    return outs[0], outs[1], key_grad, value_grad


def solution(mesh):
    split = P("ctx", "kvh")
    home = P(("ctx", "kvh"), None)
    return jax.shard_map(
        per_device,
        mesh=mesh,
        in_specs=(split, home, home, split, P()),
        out_specs=(split, split, home, home),
        check_vma=False,
    )
```

```python
import functools

import jax
import jax.numpy as jnp
from jax import lax
from jax.experimental import pallas as pl
from jax.experimental.pallas import tpu as pltpu
from jax.sharding import PartitionSpec as P

HD = 128
BLK = 128
GLOB = 2
DEPTH = 4
LOG2E = 1.4426950408889634
NN = (((1,), (0,)), ((), ()))
NT = (((1,), (1,)), ((), ()))
VMEM_LIMIT = 56 * 1024 * 1024
SMALL_VMEM = 16 * 1024 * 1024
COST = pl.CostEstimate(flops=0, bytes_accessed=1 << 10, transcendentals=0)


class Plan:
    def __init__(self, ctx, query_blocks, rand):
        self.ctx, self.qb, self.rand = ctx, query_blocks, rand
        self.sel = 3 + GLOB + rand
        self.depth = DEPTH if ctx % DEPTH == 0 else ctx
        self.lanes = ctx // self.depth
        per_owner = -(-query_blocks * rand // max(1, ctx - 4))
        most, first = 0, []
        for device in range(ctx):
            far = [s for s in range(1, ctx) if abs(s - device) > 1]
            for lane in range(self.lanes):
                there = [s for s in far if s % self.lanes == lane]
                if lane == device % self.lanes:
                    continue
                if device == 0:
                    first.append(there)
                else:
                    most = max(most, len(there))
        over = [there for there in first if len(there) > most]
        self.direct = None
        if len(over) == 1 and len(over[0]) == most + 1:
            self.direct = over[0][0]
        elif over:
            most = max(len(there) for there in over)
        self.slots = 2 + GLOB + min(query_blocks * rand, per_owner * most)
        self.direct_slots = 0 if self.direct is None else min(query_blocks, per_owner)
        self.row_slots = {}
        for step in range(1, self.depth):
            most_here = 0
            for device in range(ctx):
                row = (device // self.lanes - step) % self.depth
                inside = [s for s in range(ctx) if s // self.lanes == row]
                size = GLOB * (row == 0) + sum(abs(s - device) == 1 for s in inside)
                size += min(query_blocks * rand, per_owner * sum(s > 0 and abs(s - device) > 1 for s in inside))
                most_here = max(most_here, size)
            self.row_slots[step] = most_here
        self.own = self.depth * query_blocks
        self.far = (self.lanes - 1) * self.slots + self.direct_slots
        self.pool = self.own + self.far

    def column_place(self, me, owner, offset):
        row = lax.rem(me // self.lanes - owner // self.lanes + self.depth, self.depth)
        return row * self.qb + offset

    def place(self, me, owner, offset, slot):
        mine, theirs = lax.rem(me, self.lanes), lax.rem(owner, self.lanes)
        pack = lax.rem(theirs - mine + self.lanes, self.lanes) - 1
        return jnp.where(
            mine == theirs, self.column_place(me, owner, offset), self.own + pack * self.slots + slot
        )


def dot(a, b, dims):
    return lax.dot_general(a, b, dims, preferred_element_type=jnp.float32)


def rows_of(place):
    return pl.ds(pl.multiple_of(place * BLK, BLK), BLK)


def tables_kernel(where, named, table, walk, counts, *, plan):
    qb, rand, lanes = plan.qb, plan.rand, plan.lanes
    sel, named_each = plan.sel, plan.qb * plan.rand
    me = where[0]
    mine = lax.rem(me, lanes)
    left, right = jnp.maximum(me - 1, 0), jnp.minimum(me + 1, plan.ctx - 1)
    for lane in range(lanes):
        counts[lane] = jnp.int32(2 + GLOB)
    counts[lanes] = jnp.int32(0)
    for i in range(qb):
        table[i * sel] = plan.place(me, left, qb - 1, 0) if i == 0 else jnp.int32(i - 1)
        table[i * sel + 1] = jnp.int32(i)
        table[i * sel + 2] = plan.place(me, right, 0, 1) if i == qb - 1 else jnp.int32(i + 1)
        for j in range(GLOB):
            table[i * sel + 3 + j] = plan.place(me, jnp.int32(0), j, 2 + j)
        for j in range(3):
            block = me * qb + i - 1 + j
            counted = (block >= GLOB) & (block < plan.ctx * qb)
            table[qb * sel + i * 3 + j] = counted.astype(jnp.int32)

    def straight(device, owner):
        return jnp.bool_(False) if plan.direct is None else (device == 0) & (owner == plan.direct)

    def entry(n, carry):
        block = named[me * named_each + n]
        owner = block // qb
        apart = straight(me, owner)
        lane = jnp.where(apart, lanes, lax.rem(owner, lanes))
        slot = counts[lane]
        place = plan.place(me, owner, lax.rem(block, qb), slot)
        place = jnp.where(apart, plan.own + (lanes - 1) * plan.slots + slot, place)
        table[(n // rand) * sel + 3 + GLOB + lax.rem(n, rand)] = place
        counts[lane] = slot + 1
        return carry

    lax.fori_loop(0, named_each, entry, 0)

    def clear(n, carry):
        walk[n] = jnp.int32(0)
        return carry

    lax.fori_loop(0, plan.far, clear, 0)
    for step in range(1, lanes):
        base = (step - 1) * plan.slots
        other = me - mine + lax.rem(mine + step, lanes)

        @pl.when((other >= 1) & (lax.rem(other - 1 + lanes, lanes) == mine))
        def _():
            walk[base] = plan.column_place(me, other - 1, qb - 1)

        @pl.when((other + 1 < plan.ctx) & (lax.rem(other + 1, lanes) == mine))
        def _():
            walk[base + 1] = plan.column_place(me, other + 1, 0)

        @pl.when(mine == 0)
        def _():
            for j in range(GLOB):
                walk[base + 2 + j] = plan.column_place(me, jnp.int32(0), j)

        def theirs(n, slot):
            block = named[other * named_each + n]
            owner = block // qb
            hit = (lax.rem(owner, lanes) == mine) & jnp.logical_not(straight(other, owner))

            @pl.when(hit)
            def _():
                walk[base + slot] = plan.column_place(me, owner, lax.rem(block, qb))

            return slot + hit.astype(jnp.int32)

        lax.fori_loop(0, named_each, theirs, jnp.int32(2 + GLOB))
    if plan.direct is not None:

        @pl.when(me == plan.direct)
        def _():
            def zeroth(n, slot):
                block = named[n]
                hit = block // qb == plan.direct

                @pl.when(hit)
                def _():
                    walk[(lanes - 1) * plan.slots + slot] = lax.rem(block, qb)

                return slot + hit.astype(jnp.int32)

            lax.fori_loop(0, named_each, zeroth, jnp.int32(0))


def tables(plan, where, named):
    smem = pl.BlockSpec(memory_space=pltpu.SMEM)
    return pl.pallas_call(
        functools.partial(tables_kernel, plan=plan),
        in_specs=[smem, smem],
        out_specs=[smem, smem],
        out_shape=[
            jax.ShapeDtypeStruct((plan.qb * (plan.sel + 3),), jnp.int32),
            jax.ShapeDtypeStruct((max(1, plan.far),), jnp.int32),
        ],
        scratch_shapes=[pltpu.SMEM((plan.lanes + 1,), jnp.int32)],
        cost_estimate=COST,
        name="list_tables",
    )(where, named)


def row_tables_kernel(where, named, table, walk, counts, *, plan):
    qb, rand, lanes, depth, ctx = plan.qb, plan.rand, plan.lanes, plan.depth, plan.ctx
    sel, named_each = plan.sel, plan.qb * plan.rand
    me = where[0]
    mine, row = lax.rem(me, lanes), me // lanes

    def in_row(owner, offset):
        return lax.rem(lax.rem(owner, lanes) - mine + lanes, lanes) * qb + offset

    def walk_list(device, there, visit):
        for j in range(GLOB):
            pl.when(there == 0)(functools.partial(visit, jnp.int32(0), j, 3 + j))
        pl.when((device >= 1) & ((device - 1) // lanes == there))(functools.partial(visit, device - 1, qb - 1, 0))
        right = (device + 1 < ctx) & ((device + 1) // lanes == there)
        pl.when(right)(functools.partial(visit, device + 1, 0, (qb - 1) * sel + 2))

        def entry(n, carry):
            block = named[device * named_each + n]
            owner = block // qb
            at = (n // rand) * sel + 3 + GLOB + lax.rem(n, rand)
            pl.when(owner // lanes == there)(functools.partial(visit, owner, lax.rem(block, qb), at))
            return carry

        lax.fori_loop(0, named_each, entry, 0)

    for i in range(qb):
        table[i * sel] = jnp.int32(max(i - 1, 0))
        table[i * sel + 1] = jnp.int32(i)
        table[i * sel + 2] = jnp.int32(min(i + 1, qb - 1))

    def beside(owner, offset, at):
        table[at] = in_row(owner, offset)

    walk_list(me, row, beside)
    base, begin = lanes * qb, 0
    for step, slots in plan.row_slots.items():
        counts[0] = jnp.int32(0)

        def found(owner, offset, at, base=base):
            table[at] = base + counts[0]
            counts[0] = counts[0] + 1

        walk_list(me, lax.rem(row - step + depth, depth), found)
        counts[0] = jnp.int32(0)
        for n in range(slots):
            walk[begin + n] = jnp.int32(0)

        def asked(owner, offset, at, begin=begin):
            walk[begin + counts[0]] = in_row(owner, offset)
            counts[0] = counts[0] + 1

        walk_list(lax.rem(row + step, depth) * lanes + mine, row, asked)
        base, begin = base + slots, begin + slots
    for i in range(1, qb):
        for j in range(GLOB):
            table[i * sel + 3 + j] = table[3 + j]


def row_tables(plan, where, named):
    smem = pl.BlockSpec(memory_space=pltpu.SMEM)
    return pl.pallas_call(
        functools.partial(row_tables_kernel, plan=plan),
        in_specs=[smem, smem],
        out_specs=[smem, smem],
        out_shape=[
            jax.ShapeDtypeStruct((plan.qb * plan.sel,), jnp.int32),
            jax.ShapeDtypeStruct((sum(plan.row_slots.values()),), jnp.int32),
        ],
        scratch_shapes=[pltpu.SMEM((1,), jnp.int32)],
        cost_estimate=COST,
        name="row_tables",
    )(where, named)


def pack_rows_kernel(walk, *refs, plan):
    shards, outs, pool = refs[: plan.lanes], refs[-plan.depth : -1], refs[-1]
    rows = plan.qb * BLK
    for t in range(2):
        for lane, shard in enumerate(shards):
            pool[lane * rows : (lane + 1) * rows, :] = shard[t * rows : (t + 1) * rows, :]
        begin = 0
        for out, slots in zip(outs, plan.row_slots.values()):
            for slot in range(slots):
                place = rows_of(walk[begin + slot])
                out[(t * slots + slot) * BLK : (t * slots + slot + 1) * BLK, :] = pool[place, :]
            begin += slots


def pack_rows(plan, walk, shards, waits):
    shapes = [jax.ShapeDtypeStruct((2 * slots * BLK, HD), jnp.bfloat16) for slots in plan.row_slots.values()]
    return pl.pallas_call(
        functools.partial(pack_rows_kernel, plan=plan),
        grid_spec=pltpu.PrefetchScalarGridSpec(
            num_scalar_prefetch=1,
            grid=(1,),
            in_specs=[whole(a) for a in shards] + [ANYWHERE] * len(waits),
            out_specs=[whole(s) for s in shapes],
            scratch_shapes=[pltpu.VMEM((plan.lanes * plan.qb * BLK, HD), jnp.bfloat16)],
        ),
        out_shape=shapes,
        compiler_params=pltpu.CompilerParams(vmem_limit_bytes=SMALL_VMEM),
        cost_estimate=COST,
        name="pack_rows",
    )(walk, *shards, *waits)


def whole(a):
    return pl.BlockSpec(a.shape, lambda n, *_: (0, 0))


ANYWHERE = pl.BlockSpec(memory_space=pl.ANY)


def gate_kernel(*refs):
    del refs


def gate(array, *waits):
    return pl.pallas_call(
        gate_kernel,
        in_specs=[ANYWHERE] * (1 + len(waits)),
        out_specs=ANYWHERE,
        out_shape=jax.ShapeDtypeStruct(array.shape, array.dtype),
        input_output_aliases={0: 0},
        cost_estimate=COST,
        name="gate",
    )(array, *waits)


def pack_kernel(walk, *refs, plan, sources, base, slots, size):
    out, pool = refs[-2:]
    rows = plan.qb * BLK
    for t, some in enumerate(sources):
        for k, (n, at) in enumerate(some):
            pool[k * rows : (k + 1) * rows, :] = refs[n][at : at + rows, :]
        for slot in range(slots):
            place = walk[base + slot]
            out[(t * slots + slot) * BLK : (t * slots + slot + 1) * BLK, :] = pool[rows_of(place), :]


def pack(plan, walk, units, step, waits=()):
    rows = plan.qb * BLK
    arrays = [a for unit in units for a in (unit if step else unit[:1])]
    per = plan.depth if step else 1
    halves = units[0][0].shape[0] // rows
    sources = [
        [(u * per + k, half * rows) for k in range(per)] for u in range(len(units)) for half in range(halves)
    ]
    slots = plan.slots if step else plan.direct_slots
    base = (step - 1 if step else plan.lanes - 1) * plan.slots
    size = len(sources) * slots * BLK
    return pl.pallas_call(
        functools.partial(pack_kernel, plan=plan, sources=sources, base=base, slots=slots, size=size),
        grid_spec=pltpu.PrefetchScalarGridSpec(
            num_scalar_prefetch=1,
            grid=(1,),
            in_specs=[whole(a) for a in arrays] + [ANYWHERE] * len(waits),
            out_specs=pl.BlockSpec((size, HD), lambda n, *_: (0, 0)),
            scratch_shapes=[pltpu.VMEM((per * rows, HD), jnp.bfloat16)],
        ),
        out_shape=jax.ShapeDtypeStruct((size, HD), jnp.bfloat16),
        compiler_params=pltpu.CompilerParams(vmem_limit_bytes=SMALL_VMEM),
        cost_estimate=COST,
        name="pack_blocks",
    )(walk, *arrays, *waits)


def merge_kernel(walk, *refs, plan, halves, direct_first):
    rows = plan.qb * BLK
    columns, refs = refs[:halves], refs[halves:]
    packs, refs = refs[: halves * (plan.lanes - 1)], refs[halves * (plan.lanes - 1) :]
    direct = refs[0]
    outs, total = refs[-1 - plan.depth : -1], refs[-1]
    for t in range(halves):
        total[...] = columns[t][...].astype(jnp.float32)

        def add(given, slots, first, base):
            for slot in range(slots):
                at = (first + slot) * BLK
                total[rows_of(walk[base + slot]), :] += given[at : at + BLK, :].astype(jnp.float32)

        for step in range(1, plan.lanes):
            add(packs[t * (plan.lanes - 1) + step - 1], plan.slots, 0, (step - 1) * plan.slots)
        if plan.direct is not None:
            add(direct, plan.direct_slots, (direct_first + t) * plan.direct_slots, (plan.lanes - 1) * plan.slots)
        for k in range(plan.depth):
            outs[k][t * rows : (t + 1) * rows, :] = total[k * rows : (k + 1) * rows, :].astype(outs[k].dtype)


def merge(plan, walk, columns, packs, direct, direct_first=0, waits=()):
    halves = len(columns)
    shape = (halves * plan.qb * BLK, HD)
    kinds = [jnp.float32] + [jnp.bfloat16] * (plan.depth - 1)
    args = list(columns) + [a for some in packs for a in some] + ([] if direct is None else [direct])
    return pl.pallas_call(
        functools.partial(
            merge_kernel, plan=plan, halves=halves, direct_first=direct_first
        ),
        grid_spec=pltpu.PrefetchScalarGridSpec(
            num_scalar_prefetch=1,
            grid=(1,),
            in_specs=[whole(a) for a in args] + [ANYWHERE] * len(waits),
            out_specs=[pl.BlockSpec(shape, lambda n, *_: (0, 0))] * plan.depth,
            scratch_shapes=[pltpu.VMEM((plan.own * BLK, HD), jnp.float32)],
        ),
        out_shape=[jax.ShapeDtypeStruct(shape, kind) for kind in kinds],
        compiler_params=pltpu.CompilerParams(vmem_limit_bytes=VMEM_LIMIT),
        cost_estimate=COST,
        name="merge_terms",
    )(walk, *args, *waits)


def attend_kernel(found, table, *refs, plan, qpk, per, given, sources, split, first, ends):
    q_ref, do_ref = refs[:2]
    parts, refs = refs[2 : 2 + given], refs[2 + given :]
    before = refs[: 2 if first else 0]
    if ends:
        refs = refs[-(14 + (2 if split else 1) * (plan.lanes - 1) + (plan.direct is not None)) :]
        o_ref, dq_ref, dk_out, dv_out = refs[:4]
        packed, refs = refs[4:-10], refs[-10:]
        kpool, vpool, keys, values, dk_sum, dv_sum, dk_far, dv_far, dk_col, dv_col = refs
    else:
        o_ref, dq_ref, dk_sum, dv_sum, kpool, vpool, keys, values = refs[-8:]
    n = pl.program_id(0)
    i = n + first
    sel = plan.sel
    scale = HD ** -0.5

    def add(i, k_terms, v_terms, base):
        for j in range(sel):
            place = table[i * sel + j]
            part = slice(base + j * BLK, base + (j + 1) * BLK)

            @pl.when(place < plan.own)
            def _():
                dk_col[rows_of(place), :] += k_terms[part, :]
                dv_col[rows_of(place), :] += v_terms[part, :]

            @pl.when(place >= plan.own)
            def _():
                dk_far[rows_of(place - plan.own), :] += k_terms[part, :]
                dv_far[rows_of(place - plan.own), :] += v_terms[part, :]

    @pl.when(n == 0)
    def _():
        for pool, some in zip((kpool, vpool), sources):
            at = 0
            for source, start, size in some:
                pool[at : at + size, :] = parts[source][start : start + size, :]
                at += size
        if ends:
            for total in (dk_col, dv_col, dk_far, dv_far):
                total[...] = jnp.zeros_like(total)
        for done in range(first):
            add(done, *before, done * sel * BLK)

    for j in range(sel):
        place = rows_of(found[i * sel + j])
        keys[j * BLK : (j + 1) * BLK, :] = kpool[place, :]
        values[j * BLK : (j + 1) * BLK, :] = vpool[place, :]
    counted = [table[plan.qb * sel + i * 3 + j] != 0 for j in range(3)]
    K, V = keys[...], values[...]
    KT, VT = K.T, V.T
    for h in range(0, qpk, per):

        def stacked(ref):
            return jnp.concatenate([ref[:, (h + t) * HD : (h + t + 1) * HD] for t in range(per)], axis=0)

        q, do = stacked(q_ref), stacked(do_ref)
        scores = dot(K, q, NT)
        scores = jnp.concatenate(
            [jnp.where(counted[j], scores[j * BLK : (j + 1) * BLK], -jnp.inf) for j in range(3)]
            + [scores[3 * BLK :]],
            axis=0,
        )
        largest = jnp.max(scores, axis=0, keepdims=True)
        raised = jnp.exp2((scores - largest) * (scale * LOG2E))
        inverse = 1.0 / jnp.sum(raised, axis=0, keepdims=True)
        raised_b = raised.astype(jnp.bfloat16)
        attended = dot(VT, raised_b, NN) * inverse
        prob_grad = dot(V, do, NT)
        do_t, q_t = do.T.astype(jnp.float32), q.T.astype(jnp.float32)
        centre = jnp.sum(attended * do_t, axis=0, keepdims=True)
        score_grad = (raised * (prob_grad - centre)).astype(jnp.bfloat16)
        query_grad = dot(KT, score_grad, NN) * (inverse * scale)
        value_grad = dot(raised_b, (do_t * inverse).astype(jnp.bfloat16), NT)
        key_grad = dot(score_grad, (q_t * (inverse * scale)).astype(jnp.bfloat16), NT)
        attended, query_grad = attended.T, query_grad.T
        for t in range(per):
            o_ref[:, (h + t) * HD : (h + t + 1) * HD] = attended[t * BLK : (t + 1) * BLK].astype(jnp.bfloat16)
            dq_ref[:, (h + t) * HD : (h + t + 1) * HD] = query_grad[t * BLK : (t + 1) * BLK].astype(jnp.bfloat16)
        if h == 0:
            dk_sum[...], dv_sum[...] = key_grad, value_grad
        else:
            dk_sum[...] += key_grad
            dv_sum[...] += value_grad
    if not ends:
        return
    add(i, dk_sum, dv_sum, 0)

    @pl.when(i == plan.qb - 1)
    def _():
        dk_out[...] = dk_col[...].astype(jnp.bfloat16)
        dv_out[...] = dv_col[...].astype(jnp.bfloat16)
        size = plan.slots * BLK
        for t in range(plan.lanes - 1):
            part = slice(t * size, (t + 1) * size)
            if split:
                packed[t][...] = dk_far[part, :].astype(jnp.bfloat16)
                packed[plan.lanes - 1 + t][...] = dv_far[part, :].astype(jnp.bfloat16)
            else:
                packed[t][:size, :] = dk_far[part, :].astype(jnp.bfloat16)
                packed[t][size:, :] = dv_far[part, :].astype(jnp.bfloat16)
        if plan.direct is not None:
            rest = slice((plan.lanes - 1) * size, plan.far * BLK)
            packed[-1][: plan.direct_slots * BLK, :] = dk_far[rest, :].astype(jnp.bfloat16)
            packed[-1][plan.direct_slots * BLK :, :] = dv_far[rest, :].astype(jnp.bfloat16)


def attend(plan, found, table, queries, out_grad, pieces, group, qpk, outs, split, first, count, terms=(), waits=()):
    width = qpk * HD
    parts, sources = [], [[], []]
    for array, kind, step in pieces:
        for half in range(2):
            if kind == half:
                sources[half].append((len(parts), 0, step))
            elif kind == 2:
                sources[half] += [(len(parts), at + half * step, step) for at in range(0, array.shape[0], 2 * step)]
        parts.append(array)
    pool = pltpu.VMEM((sum(step for _, _, step in sources[0]), HD), jnp.bfloat16)
    q_spec = pl.BlockSpec((BLK, width), lambda n, *_: (n + first, group))
    shape = lambda blocks, kind: jax.ShapeDtypeStruct((blocks * BLK, HD), kind)
    o_shape = jax.ShapeDtypeStruct(queries.shape, jnp.bfloat16)
    ends = first + count == plan.qb
    term_shape = shape(plan.own, jnp.bfloat16) if ends else shape(count * plan.sel, jnp.float32)
    out_shape = [o_shape, o_shape, term_shape, term_shape]
    if ends:
        out_shape += [shape((1 if split else 2) * plan.slots, jnp.bfloat16)] * ((2 if split else 1) * (plan.lanes - 1))
    if ends and plan.direct is not None:
        out_shape.append(shape(2 * plan.direct_slots, jnp.bfloat16))
    args = [queries, out_grad, *parts, *terms]
    in_specs = [q_spec, q_spec] + [whole(a) for a in args[2:]]
    aliases = {2 + len(args) + t: t for t in range(len(outs))}
    listed = pltpu.VMEM((plan.sel * BLK, HD), jnp.bfloat16)
    term_spec = pl.BlockSpec((plan.sel * BLK, HD), lambda n, *_: (n, 0))
    listed_sum = pltpu.VMEM((plan.sel * BLK, HD), jnp.float32)
    out = pl.pallas_call(
        functools.partial(
            attend_kernel, plan=plan, qpk=qpk, per=4 if qpk % 4 == 0 else 1, given=len(parts), sources=sources, split=split,
            first=first, ends=ends,
        ),
        grid_spec=pltpu.PrefetchScalarGridSpec(
            num_scalar_prefetch=2,
            grid=(count,),
            in_specs=in_specs + [ANYWHERE] * (len(outs) + len(waits)),
            out_specs=[q_spec, q_spec] + ([whole(s) for s in out_shape[2:]] if ends else [term_spec] * 2),
            scratch_shapes=[pool] * 2
            + [listed, listed]
            + ([listed_sum, listed_sum] + [pltpu.VMEM((blocks * BLK, HD), jnp.float32) for blocks in (plan.far, plan.far, plan.own, plan.own)] if ends else []),
        ),
        out_shape=out_shape,
        input_output_aliases=aliases,
        compiler_params=pltpu.CompilerParams(vmem_limit_bytes=VMEM_LIMIT),
        cost_estimate=COST,
        name="attend_head",
    )(found, table, *args, *outs, *waits)
    outs, columns, far = out[:2], out[2:4], list(out[4:])
    if not ends:
        return outs, columns, None
    straight = far.pop() if plan.direct is not None else None
    return outs, columns, ([far[: plan.lanes - 1], far[plan.lanes - 1 :]] if split else [far], straight)


def column_shift(array, plan, rows):
    return lax.ppermute(array, "ctx", [(n, (n + rows * plan.lanes) % plan.ctx) for n in range(plan.ctx)])


def row_shift(array, plan, lanes):
    return lax.ppermute(
        array, "ctx", [(n, n - n % plan.lanes + (n + lanes) % plan.lanes) for n in range(plan.ctx)]
    )


def straight_shift(array, plan, there, back):
    return lax.ppermute(array, "ctx", [(there, back)])


def cut_kernel(keys, values, out, *, size, groups):
    for n in range(size):
        for g in range(groups):
            part = slice((n * groups + g) * HD, (n * groups + g + 1) * HD)
            out[n, 2 * g] = keys[:, part]
            out[n, 2 * g + 1] = values[:, part]


def join_kernel(parts, *outs, size, groups):
    rows = parts.shape[2]
    for n in range(size):
        for g in range(groups):
            for t in range(2):
                out, at = (outs[t], 0) if g == 0 else (outs[1 + g], t * size * rows)
                out[at + n * rows : at + (n + 1) * rows, :] = parts[n, 2 * g + t]


def to_heads(keys, values, groups):
    size = lax.axis_size("kvh")
    rows = keys.shape[0]
    vmem = pl.BlockSpec(memory_space=pltpu.VMEM)
    parts = pl.pallas_call(
        functools.partial(cut_kernel, size=size, groups=groups),
        in_specs=[vmem, vmem],
        out_specs=vmem,
        out_shape=jax.ShapeDtypeStruct((size, 2 * groups, rows, HD), keys.dtype),
        cost_estimate=COST,
        name="cut_heads",
    )(keys, values)
    parts = lax.all_to_all(parts, "kvh", split_axis=0, concat_axis=0, tiled=True)
    shapes = [(size * rows, HD)] * 2 + [(2 * size * rows, HD)] * (groups - 1)
    return pl.pallas_call(
        functools.partial(join_kernel, size=size, groups=groups),
        in_specs=[vmem],
        out_specs=[vmem] * len(shapes),
        out_shape=[jax.ShapeDtypeStruct(shape, keys.dtype) for shape in shapes],
        cost_estimate=COST,
        name="join_heads",
    )(parts)


def to_tokens(array, count):
    size = lax.axis_size("kvh")
    parts = jnp.moveaxis(array.reshape(count, size, -1, HD), 1, 0)
    parts = lax.all_to_all(parts, "kvh", split_axis=0, concat_axis=0, tiled=True)
    return [parts[:, t] for t in range(count)]


def per_device(queries, keys, values, out_grad, random_blocks):
    kvh = lax.axis_size("kvh")
    groups = keys.shape[1] // (kvh * HD)
    qpk = queries.shape[1] // (groups * HD)
    plan = Plan(lax.axis_size("ctx"), queries.shape[0] // BLK, random_blocks.shape[1])
    lanes, depth, qb = plan.lanes, plan.depth, plan.qb
    where = lax.axis_index("ctx").astype(jnp.int32).reshape(1)
    table, walk = tables(plan, where, random_blocks.reshape(-1))

    def spread(own):
        return [own] + [column_shift(own, plan, k) for k in range(1, depth)]

    def across(units, waits=()):
        return [row_shift(pack(plan, walk, units, lanes - t, waits), plan, lanes - t) for t in range(1, lanes)]

    def straight(units, waits=()):
        if plan.direct is None:
            return None
        return straight_shift(pack(plan, walk, units, 0, waits), plan, plan.direct, 0)

    def send_back(packs):
        return [row_shift(packs[t - 1], plan, t) for t in range(1, lanes)][::-1]

    def home(terms, count):
        arrived = [column_shift(terms[k], plan, depth - k) for k in range(1, depth)]
        total = terms[0]
        for array in arrived:
            total = total + array.astype(jnp.float32)
        return to_tokens(total.astype(jnp.bfloat16), count), arrived

    rows, size = qb * BLK, plan.slots * BLK
    own = to_heads(keys, values, groups)
    own, joined = own[:2], own[2:]
    units = [spread(a) for a in own]
    direct = straight([[a] for a in own], tuple(units[0][1:]))
    in_row = [[a] + [row_shift(a, plan, lanes - t) for t in range(1, lanes)] for a in joined]
    packs = [across([units[0]], tuple(a for some in in_row for a in some[1:]))]
    packs.append(across([units[1]], (*packs[0], *([] if direct is None else [direct]))))
    pieces = [(a, t, rows) for t in range(2) for a in units[t]] + [(a, t, size) for t in range(2) for a in packs[t]]
    if direct is not None:
        pieces.append((direct, 2, plan.direct_slots * BLK))
    ready = [a for unit in units for a in unit[1:]]
    found, homes, outs, arrived, waits = table, [], [], [], ()
    if groups > 1:
        row_found, row_walk = row_tables(plan, where, random_blocks.reshape(-1))
    for g in range(groups):
        last = g + 1 == groups
        if not last:
            sent = pack_rows(plan, row_walk, in_row[g], tuple(ready))
            waits = (sent[0],)
            ready = [column_shift(a, plan, step) for a, step in zip(sent, plan.row_slots)]
        run = functools.partial(attend, plan, found, table, queries, out_grad, pieces, g, qpk)
        if not g:
            outs, columns, (far, far_direct) = run(outs, True, 0, qb, (), waits)
        else:
            before = merge(plan, walk, *before, waits=tuple(a for a, _, _ in pieces))
            total, arrived = home(before, 2)
            homes.append(total)
            outs, columns, (far, far_direct) = run(outs, True, 0, qb, (), (before[1],))
        if arrived:
            far[1] = [gate(a, *arrived) for a in far[1]]
            far_direct = far_direct if far_direct is None else gate(far_direct, *arrived)
        if far_direct is not None:
            far_direct = straight_shift(far_direct, plan, 0, plan.direct)
        backs = [send_back(some) for some in far]
        if last:
            for t in range(2):
                terms = merge(plan, walk, [columns[t]], [backs[t]], far_direct, direct_first=t)
                homes.append(home(terms, 1)[0])
        else:
            before = columns, backs, far_direct
            found, pieces = row_found, [(a, 2, rows) for a in in_row[g]]
            pieces += [(a, 2, slots * BLK) for a, slots in zip(ready, plan.row_slots.values())]
    homes[-2:] = [homes[-2] + homes[-1]]
    key_grad, value_grad = (
        jnp.stack([some[n] for some in homes], axis=2).transpose(1, 0, 2, 3).reshape(keys.shape) for n in range(2)
    )
    return outs[0], outs[1], key_grad, value_grad


def solution(mesh):
    split = P("ctx", "kvh")
    home = P(("ctx", "kvh"), None)
    return jax.shard_map(
        per_device,
        mesh=mesh,
        in_specs=(split, home, home, split, P()),
        out_specs=(split, split, home, home),
        check_vma=False,
    )
```

```python
import functools

import jax
import jax.numpy as jnp
from jax import lax
from jax.experimental import pallas as pl
from jax.experimental.pallas import tpu as pltpu
from jax.sharding import PartitionSpec as P

HD = 128
BLK = 128
GLOB = 2
DEPTH = 4
LOG2E = 1.4426950408889634
NN = (((1,), (0,)), ((), ()))
NT = (((1,), (1,)), ((), ()))
VMEM_LIMIT = 56 * 1024 * 1024
SMALL_VMEM = 16 * 1024 * 1024
COST = pl.CostEstimate(flops=0, bytes_accessed=1 << 10, transcendentals=0)


class Plan:
    def __init__(self, ctx, query_blocks, rand):
        self.ctx, self.qb, self.rand = ctx, query_blocks, rand
        self.sel = 3 + GLOB + rand
        self.depth = DEPTH if ctx % DEPTH == 0 else ctx
        self.lanes = ctx // self.depth
        per_owner = -(-query_blocks * rand // max(1, ctx - 4))
        most, first = 0, []
        for device in range(ctx):
            far = [s for s in range(1, ctx) if abs(s - device) > 1]
            for lane in range(self.lanes):
                there = [s for s in far if s % self.lanes == lane]
                if lane == device % self.lanes:
                    continue
                if device == 0:
                    first.append(there)
                else:
                    most = max(most, len(there))
        over = [there for there in first if len(there) > most]
        self.direct = None
        if len(over) == 1 and len(over[0]) == most + 1:
            self.direct = over[0][0]
        elif over:
            most = max(len(there) for there in over)
        self.slots = 2 + GLOB + min(query_blocks * rand, per_owner * most)
        self.direct_slots = 0 if self.direct is None else min(query_blocks, per_owner)
        self.row_slots = {}
        for step in range(1, self.depth):
            most_here = 0
            for device in range(ctx):
                row = (device // self.lanes - step) % self.depth
                inside = [s for s in range(ctx) if s // self.lanes == row]
                size = GLOB * (row == 0) + sum(abs(s - device) == 1 for s in inside)
                size += min(query_blocks * rand, per_owner * sum(s > 0 and abs(s - device) > 1 for s in inside))
                most_here = max(most_here, size)
            self.row_slots[step] = most_here
        self.own = self.depth * query_blocks
        self.far = (self.lanes - 1) * self.slots + self.direct_slots
        self.pool = self.own + self.far

    def column_place(self, me, owner, offset):
        row = lax.rem(me // self.lanes - owner // self.lanes + self.depth, self.depth)
        return row * self.qb + offset

    def place(self, me, owner, offset, slot):
        mine, theirs = lax.rem(me, self.lanes), lax.rem(owner, self.lanes)
        pack = lax.rem(theirs - mine + self.lanes, self.lanes) - 1
        return jnp.where(
            mine == theirs, self.column_place(me, owner, offset), self.own + pack * self.slots + slot
        )


def dot(a, b, dims):
    return lax.dot_general(a, b, dims, preferred_element_type=jnp.float32)


def rows_of(place):
    return pl.ds(pl.multiple_of(place * BLK, BLK), BLK)


def tables_kernel(where, named, table, walk, counts, *, plan):
    qb, rand, lanes = plan.qb, plan.rand, plan.lanes
    sel, named_each = plan.sel, plan.qb * plan.rand
    me = where[0]
    mine = lax.rem(me, lanes)
    left, right = jnp.maximum(me - 1, 0), jnp.minimum(me + 1, plan.ctx - 1)
    for lane in range(lanes):
        counts[lane] = jnp.int32(2 + GLOB)
    counts[lanes] = jnp.int32(0)
    for i in range(qb):
        table[i * sel] = plan.place(me, left, qb - 1, 0) if i == 0 else jnp.int32(i - 1)
        table[i * sel + 1] = jnp.int32(i)
        table[i * sel + 2] = plan.place(me, right, 0, 1) if i == qb - 1 else jnp.int32(i + 1)
        for j in range(GLOB):
            table[i * sel + 3 + j] = plan.place(me, jnp.int32(0), j, 2 + j)
        for j in range(3):
            block = me * qb + i - 1 + j
            counted = (block >= GLOB) & (block < plan.ctx * qb)
            table[qb * sel + i * 3 + j] = counted.astype(jnp.int32)

    def straight(device, owner):
        return jnp.bool_(False) if plan.direct is None else (device == 0) & (owner == plan.direct)

    def entry(n, carry):
        block = named[me * named_each + n]
        owner = block // qb
        apart = straight(me, owner)
        lane = jnp.where(apart, lanes, lax.rem(owner, lanes))
        slot = counts[lane]
        place = plan.place(me, owner, lax.rem(block, qb), slot)
        place = jnp.where(apart, plan.own + (lanes - 1) * plan.slots + slot, place)
        table[(n // rand) * sel + 3 + GLOB + lax.rem(n, rand)] = place
        counts[lane] = slot + 1
        return carry

    lax.fori_loop(0, named_each, entry, 0)

    def clear(n, carry):
        walk[n] = jnp.int32(0)
        return carry

    lax.fori_loop(0, plan.far, clear, 0)
    for step in range(1, lanes):
        base = (step - 1) * plan.slots
        other = me - mine + lax.rem(mine + step, lanes)

        @pl.when((other >= 1) & (lax.rem(other - 1 + lanes, lanes) == mine))
        def _():
            walk[base] = plan.column_place(me, other - 1, qb - 1)

        @pl.when((other + 1 < plan.ctx) & (lax.rem(other + 1, lanes) == mine))
        def _():
            walk[base + 1] = plan.column_place(me, other + 1, 0)

        @pl.when(mine == 0)
        def _():
            for j in range(GLOB):
                walk[base + 2 + j] = plan.column_place(me, jnp.int32(0), j)

        def theirs(n, slot):
            block = named[other * named_each + n]
            owner = block // qb
            hit = (lax.rem(owner, lanes) == mine) & jnp.logical_not(straight(other, owner))

            @pl.when(hit)
            def _():
                walk[base + slot] = plan.column_place(me, owner, lax.rem(block, qb))

            return slot + hit.astype(jnp.int32)

        lax.fori_loop(0, named_each, theirs, jnp.int32(2 + GLOB))
    if plan.direct is not None:

        @pl.when(me == plan.direct)
        def _():
            def zeroth(n, slot):
                block = named[n]
                hit = block // qb == plan.direct

                @pl.when(hit)
                def _():
                    walk[(lanes - 1) * plan.slots + slot] = lax.rem(block, qb)

                return slot + hit.astype(jnp.int32)

            lax.fori_loop(0, named_each, zeroth, jnp.int32(0))


def tables(plan, where, named):
    smem = pl.BlockSpec(memory_space=pltpu.SMEM)
    return pl.pallas_call(
        functools.partial(tables_kernel, plan=plan),
        in_specs=[smem, smem],
        out_specs=[smem, smem],
        out_shape=[
            jax.ShapeDtypeStruct((plan.qb * (plan.sel + 3),), jnp.int32),
            jax.ShapeDtypeStruct((max(1, plan.far),), jnp.int32),
        ],
        scratch_shapes=[pltpu.SMEM((plan.lanes + 1,), jnp.int32)],
        cost_estimate=COST,
        name="list_tables",
    )(where, named)


def row_tables_kernel(where, named, table, walk, counts, *, plan):
    qb, rand, lanes, depth, ctx = plan.qb, plan.rand, plan.lanes, plan.depth, plan.ctx
    sel, named_each = plan.sel, plan.qb * plan.rand
    me = where[0]
    mine, row = lax.rem(me, lanes), me // lanes

    def in_row(owner, offset):
        return lax.rem(lax.rem(owner, lanes) - mine + lanes, lanes) * qb + offset

    def walk_list(device, there, visit):
        for j in range(GLOB):
            pl.when(there == 0)(functools.partial(visit, jnp.int32(0), j, 3 + j))
        pl.when((device >= 1) & ((device - 1) // lanes == there))(functools.partial(visit, device - 1, qb - 1, 0))
        right = (device + 1 < ctx) & ((device + 1) // lanes == there)
        pl.when(right)(functools.partial(visit, device + 1, 0, (qb - 1) * sel + 2))

        def entry(n, carry):
            block = named[device * named_each + n]
            owner = block // qb
            at = (n // rand) * sel + 3 + GLOB + lax.rem(n, rand)
            pl.when(owner // lanes == there)(functools.partial(visit, owner, lax.rem(block, qb), at))
            return carry

        lax.fori_loop(0, named_each, entry, 0)

    for i in range(qb):
        table[i * sel] = jnp.int32(max(i - 1, 0))
        table[i * sel + 1] = jnp.int32(i)
        table[i * sel + 2] = jnp.int32(min(i + 1, qb - 1))

    def beside(owner, offset, at):
        table[at] = in_row(owner, offset)

    walk_list(me, row, beside)
    base, begin = lanes * qb, 0
    for step, slots in plan.row_slots.items():
        counts[0] = jnp.int32(0)

        def found(owner, offset, at, base=base):
            table[at] = base + counts[0]
            counts[0] = counts[0] + 1

        walk_list(me, lax.rem(row - step + depth, depth), found)
        counts[0] = jnp.int32(0)
        for n in range(slots):
            walk[begin + n] = jnp.int32(0)

        def asked(owner, offset, at, begin=begin):
            walk[begin + counts[0]] = in_row(owner, offset)
            counts[0] = counts[0] + 1

        walk_list(lax.rem(row + step, depth) * lanes + mine, row, asked)
        base, begin = base + slots, begin + slots
    for i in range(1, qb):
        for j in range(GLOB):
            table[i * sel + 3 + j] = table[3 + j]


def row_tables(plan, where, named):
    smem = pl.BlockSpec(memory_space=pltpu.SMEM)
    return pl.pallas_call(
        functools.partial(row_tables_kernel, plan=plan),
        in_specs=[smem, smem],
        out_specs=[smem, smem],
        out_shape=[
            jax.ShapeDtypeStruct((plan.qb * plan.sel,), jnp.int32),
            jax.ShapeDtypeStruct((sum(plan.row_slots.values()),), jnp.int32),
        ],
        scratch_shapes=[pltpu.SMEM((1,), jnp.int32)],
        cost_estimate=COST,
        name="row_tables",
    )(where, named)


def pack_rows_kernel(walk, *refs, plan):
    shards, outs, pool = refs[: plan.lanes], refs[-plan.depth : -1], refs[-1]
    rows = plan.qb * BLK
    for t in range(2):
        for lane, shard in enumerate(shards):
            pool[lane * rows : (lane + 1) * rows, :] = shard[t * rows : (t + 1) * rows, :]
        begin = 0
        for out, slots in zip(outs, plan.row_slots.values()):
            for slot in range(slots):
                place = rows_of(walk[begin + slot])
                out[(t * slots + slot) * BLK : (t * slots + slot + 1) * BLK, :] = pool[place, :]
            begin += slots


def pack_rows(plan, walk, shards, waits):
    shapes = [jax.ShapeDtypeStruct((2 * slots * BLK, HD), jnp.bfloat16) for slots in plan.row_slots.values()]
    return pl.pallas_call(
        functools.partial(pack_rows_kernel, plan=plan),
        grid_spec=pltpu.PrefetchScalarGridSpec(
            num_scalar_prefetch=1,
            grid=(1,),
            in_specs=[whole(a) for a in shards] + [ANYWHERE] * len(waits),
            out_specs=[whole(s) for s in shapes],
            scratch_shapes=[pltpu.VMEM((plan.lanes * plan.qb * BLK, HD), jnp.bfloat16)],
        ),
        out_shape=shapes,
        compiler_params=pltpu.CompilerParams(vmem_limit_bytes=SMALL_VMEM),
        cost_estimate=COST,
        name="pack_rows",
    )(walk, *shards, *waits)


def whole(a):
    return pl.BlockSpec(a.shape, lambda n, *_: (0, 0))


ANYWHERE = pl.BlockSpec(memory_space=pl.ANY)


def gate_kernel(*refs):
    del refs


def gate(array, *waits):
    return pl.pallas_call(
        gate_kernel,
        in_specs=[ANYWHERE] * (1 + len(waits)),
        out_specs=ANYWHERE,
        out_shape=jax.ShapeDtypeStruct(array.shape, array.dtype),
        input_output_aliases={0: 0},
        cost_estimate=COST,
        name="gate",
    )(array, *waits)


def pack_kernel(walk, *refs, plan, sources, base, slots, size):
    out, pool = refs[-2:]
    rows = plan.qb * BLK
    for t, some in enumerate(sources):
        for k, (n, at) in enumerate(some):
            pool[k * rows : (k + 1) * rows, :] = refs[n][at : at + rows, :]
        for slot in range(slots):
            place = walk[base + slot]
            out[(t * slots + slot) * BLK : (t * slots + slot + 1) * BLK, :] = pool[rows_of(place), :]


def pack(plan, walk, units, step, waits=()):
    rows = plan.qb * BLK
    arrays = [a for unit in units for a in (unit if step else unit[:1])]
    per = plan.depth if step else 1
    halves = units[0][0].shape[0] // rows
    sources = [
        [(u * per + k, half * rows) for k in range(per)] for u in range(len(units)) for half in range(halves)
    ]
    slots = plan.slots if step else plan.direct_slots
    base = (step - 1 if step else plan.lanes - 1) * plan.slots
    size = len(sources) * slots * BLK
    return pl.pallas_call(
        functools.partial(pack_kernel, plan=plan, sources=sources, base=base, slots=slots, size=size),
        grid_spec=pltpu.PrefetchScalarGridSpec(
            num_scalar_prefetch=1,
            grid=(1,),
            in_specs=[whole(a) for a in arrays] + [ANYWHERE] * len(waits),
            out_specs=pl.BlockSpec((size, HD), lambda n, *_: (0, 0)),
            scratch_shapes=[pltpu.VMEM((per * rows, HD), jnp.bfloat16)],
        ),
        out_shape=jax.ShapeDtypeStruct((size, HD), jnp.bfloat16),
        compiler_params=pltpu.CompilerParams(vmem_limit_bytes=SMALL_VMEM),
        cost_estimate=COST,
        name="pack_blocks",
    )(walk, *arrays, *waits)


def merge_kernel(walk, *refs, plan, halves, direct_first):
    rows = plan.qb * BLK
    columns, refs = refs[:halves], refs[halves:]
    packs, refs = refs[: halves * (plan.lanes - 1)], refs[halves * (plan.lanes - 1) :]
    direct = refs[0]
    outs, total = refs[-1 - plan.depth : -1], refs[-1]
    for t in range(halves):
        total[...] = columns[t][...].astype(jnp.float32)

        def add(given, slots, first, base):
            for slot in range(slots):
                at = (first + slot) * BLK
                total[rows_of(walk[base + slot]), :] += given[at : at + BLK, :].astype(jnp.float32)

        for step in range(1, plan.lanes):
            add(packs[t * (plan.lanes - 1) + step - 1], plan.slots, 0, (step - 1) * plan.slots)
        if plan.direct is not None:
            add(direct, plan.direct_slots, (direct_first + t) * plan.direct_slots, (plan.lanes - 1) * plan.slots)
        for k in range(plan.depth):
            outs[k][t * rows : (t + 1) * rows, :] = total[k * rows : (k + 1) * rows, :].astype(outs[k].dtype)


def merge(plan, walk, columns, packs, direct, direct_first=0, waits=()):
    halves = len(columns)
    shape = (halves * plan.qb * BLK, HD)
    kinds = [jnp.float32] + [jnp.bfloat16] * (plan.depth - 1)
    args = list(columns) + [a for some in packs for a in some] + ([] if direct is None else [direct])
    return pl.pallas_call(
        functools.partial(
            merge_kernel, plan=plan, halves=halves, direct_first=direct_first
        ),
        grid_spec=pltpu.PrefetchScalarGridSpec(
            num_scalar_prefetch=1,
            grid=(1,),
            in_specs=[whole(a) for a in args] + [ANYWHERE] * len(waits),
            out_specs=[pl.BlockSpec(shape, lambda n, *_: (0, 0))] * plan.depth,
            scratch_shapes=[pltpu.VMEM((plan.own * BLK, HD), jnp.float32)],
        ),
        out_shape=[jax.ShapeDtypeStruct(shape, kind) for kind in kinds],
        compiler_params=pltpu.CompilerParams(vmem_limit_bytes=VMEM_LIMIT),
        cost_estimate=COST,
        name="merge_terms",
    )(walk, *args, *waits)


def attend_kernel(found, table, *refs, plan, qpk, per, given, sources, split, first, ends):
    q_ref, do_ref = refs[:2]
    parts, refs = refs[2 : 2 + given], refs[2 + given :]
    before = refs[: 2 if first else 0]
    if ends:
        refs = refs[-(14 + (2 if split else 1) * (plan.lanes - 1) + (plan.direct is not None)) :]
        o_ref, dq_ref, dk_out, dv_out = refs[:4]
        packed, refs = refs[4:-10], refs[-10:]
        kpool, vpool, keys, values, dk_sum, dv_sum, dk_far, dv_far, dk_col, dv_col = refs
    else:
        o_ref, dq_ref, dk_sum, dv_sum, kpool, vpool, keys, values = refs[-8:]
    n = pl.program_id(0)
    i = n + first
    sel = plan.sel
    scale = HD ** -0.5

    def add(i, k_terms, v_terms, base):
        for j in range(sel):
            place = table[i * sel + j]
            part = slice(base + j * BLK, base + (j + 1) * BLK)

            @pl.when(place < plan.own)
            def _():
                dk_col[rows_of(place), :] += k_terms[part, :]
                dv_col[rows_of(place), :] += v_terms[part, :]

            @pl.when(place >= plan.own)
            def _():
                dk_far[rows_of(place - plan.own), :] += k_terms[part, :]
                dv_far[rows_of(place - plan.own), :] += v_terms[part, :]

    @pl.when(n == 0)
    def _():
        for pool, some in zip((kpool, vpool), sources):
            at = 0
            for source, start, size in some:
                pool[at : at + size, :] = parts[source][start : start + size, :]
                at += size
        if ends:
            for total in (dk_col, dv_col, dk_far, dv_far):
                total[...] = jnp.zeros_like(total)
        for done in range(first):
            add(done, *before, done * sel * BLK)

    for j in range(sel):
        place = rows_of(found[i * sel + j])
        keys[j * BLK : (j + 1) * BLK, :] = kpool[place, :]
        values[j * BLK : (j + 1) * BLK, :] = vpool[place, :]
    counted = [table[plan.qb * sel + i * 3 + j] != 0 for j in range(3)]
    K, V = keys[...], values[...]
    KT, VT = K.T, V.T
    for h in range(0, qpk, per):

        def stacked(ref):
            return jnp.concatenate([ref[:, (h + t) * HD : (h + t + 1) * HD] for t in range(per)], axis=0)

        q, do = stacked(q_ref), stacked(do_ref)
        scores = dot(K, q, NT)
        scores = jnp.concatenate(
            [jnp.where(counted[j], scores[j * BLK : (j + 1) * BLK], -jnp.inf) for j in range(3)]
            + [scores[3 * BLK :]],
            axis=0,
        )
        largest = jnp.max(scores, axis=0, keepdims=True)
        raised = jnp.exp2((scores - largest) * (scale * LOG2E))
        inverse = 1.0 / jnp.sum(raised, axis=0, keepdims=True)
        raised_b = raised.astype(jnp.bfloat16)
        attended = dot(VT, raised_b, NN) * inverse
        prob_grad = dot(V, do, NT)
        do_t, q_t = do.T.astype(jnp.float32), q.T.astype(jnp.float32)
        centre = jnp.sum(attended * do_t, axis=0, keepdims=True)
        score_grad = (raised * (prob_grad - centre)).astype(jnp.bfloat16)
        query_grad = dot(KT, score_grad, NN) * (inverse * scale)
        value_grad = dot(raised_b, (do_t * inverse).astype(jnp.bfloat16), NT)
        key_grad = dot(score_grad, (q_t * (inverse * scale)).astype(jnp.bfloat16), NT)
        attended, query_grad = attended.T, query_grad.T
        for t in range(per):
            o_ref[:, (h + t) * HD : (h + t + 1) * HD] = attended[t * BLK : (t + 1) * BLK].astype(jnp.bfloat16)
            dq_ref[:, (h + t) * HD : (h + t + 1) * HD] = query_grad[t * BLK : (t + 1) * BLK].astype(jnp.bfloat16)
        if h == 0:
            dk_sum[...], dv_sum[...] = key_grad, value_grad
        else:
            dk_sum[...] += key_grad
            dv_sum[...] += value_grad
    if not ends:
        return
    add(i, dk_sum, dv_sum, 0)

    @pl.when(i == plan.qb - 1)
    def _():
        dk_out[...] = dk_col[...].astype(jnp.bfloat16)
        dv_out[...] = dv_col[...].astype(jnp.bfloat16)
        size = plan.slots * BLK
        for t in range(plan.lanes - 1):
            part = slice(t * size, (t + 1) * size)
            if split:
                packed[t][...] = dk_far[part, :].astype(jnp.bfloat16)
                packed[plan.lanes - 1 + t][...] = dv_far[part, :].astype(jnp.bfloat16)
            else:
                packed[t][:size, :] = dk_far[part, :].astype(jnp.bfloat16)
                packed[t][size:, :] = dv_far[part, :].astype(jnp.bfloat16)
        if plan.direct is not None:
            rest = slice((plan.lanes - 1) * size, plan.far * BLK)
            packed[-1][: plan.direct_slots * BLK, :] = dk_far[rest, :].astype(jnp.bfloat16)
            packed[-1][plan.direct_slots * BLK :, :] = dv_far[rest, :].astype(jnp.bfloat16)


def attend(plan, found, table, queries, out_grad, pieces, group, qpk, outs, split, first, count, terms=(), waits=()):
    width = qpk * HD
    parts, sources = [], [[], []]
    for array, kind, step in pieces:
        for half in range(2):
            if kind == half:
                sources[half].append((len(parts), 0, step))
            elif kind == 2:
                sources[half] += [(len(parts), at + half * step, step) for at in range(0, array.shape[0], 2 * step)]
        parts.append(array)
    pool = pltpu.VMEM((sum(step for _, _, step in sources[0]), HD), jnp.bfloat16)
    q_spec = pl.BlockSpec((BLK, width), lambda n, *_: (n + first, group))
    shape = lambda blocks, kind: jax.ShapeDtypeStruct((blocks * BLK, HD), kind)
    o_shape = jax.ShapeDtypeStruct(queries.shape, jnp.bfloat16)
    ends = first + count == plan.qb
    term_shape = shape(plan.own, jnp.bfloat16) if ends else shape(count * plan.sel, jnp.float32)
    out_shape = [o_shape, o_shape, term_shape, term_shape]
    if ends:
        out_shape += [shape((1 if split else 2) * plan.slots, jnp.bfloat16)] * ((2 if split else 1) * (plan.lanes - 1))
    if ends and plan.direct is not None:
        out_shape.append(shape(2 * plan.direct_slots, jnp.bfloat16))
    args = [queries, out_grad, *parts, *terms]
    in_specs = [q_spec, q_spec] + [whole(a) for a in args[2:]]
    aliases = {2 + len(args) + t: t for t in range(len(outs))}
    listed = pltpu.VMEM((plan.sel * BLK, HD), jnp.bfloat16)
    term_spec = pl.BlockSpec((plan.sel * BLK, HD), lambda n, *_: (n, 0))
    listed_sum = pltpu.VMEM((plan.sel * BLK, HD), jnp.float32)
    out = pl.pallas_call(
        functools.partial(
            attend_kernel, plan=plan, qpk=qpk, per=4 if qpk % 4 == 0 else 1, given=len(parts), sources=sources, split=split,
            first=first, ends=ends,
        ),
        grid_spec=pltpu.PrefetchScalarGridSpec(
            num_scalar_prefetch=2,
            grid=(count,),
            in_specs=in_specs + [ANYWHERE] * (len(outs) + len(waits)),
            out_specs=[q_spec, q_spec] + ([whole(s) for s in out_shape[2:]] if ends else [term_spec] * 2),
            scratch_shapes=[pool] * 2
            + [listed, listed]
            + ([listed_sum, listed_sum] + [pltpu.VMEM((blocks * BLK, HD), jnp.float32) for blocks in (plan.far, plan.far, plan.own, plan.own)] if ends else []),
        ),
        out_shape=out_shape,
        input_output_aliases=aliases,
        compiler_params=pltpu.CompilerParams(vmem_limit_bytes=VMEM_LIMIT),
        cost_estimate=COST,
        name="attend_head",
    )(found, table, *args, *outs, *waits)
    outs, columns, far = out[:2], out[2:4], list(out[4:])
    if not ends:
        return outs, columns, None
    straight = far.pop() if plan.direct is not None else None
    return outs, columns, ([far[: plan.lanes - 1], far[plan.lanes - 1 :]] if split else [far], straight)


def column_shift(array, plan, rows):
    return lax.ppermute(array, "ctx", [(n, (n + rows * plan.lanes) % plan.ctx) for n in range(plan.ctx)])


def row_shift(array, plan, lanes):
    return lax.ppermute(
        array, "ctx", [(n, n - n % plan.lanes + (n + lanes) % plan.lanes) for n in range(plan.ctx)]
    )


def straight_shift(array, plan, there, back):
    return lax.ppermute(array, "ctx", [(there, back)])


def cut_kernel(keys, values, out, *, size, groups):
    for n in range(size):
        for g in range(groups):
            part = slice((n * groups + g) * HD, (n * groups + g + 1) * HD)
            out[n, 2 * g] = keys[:, part]
            out[n, 2 * g + 1] = values[:, part]


def join_kernel(parts, *outs, size, groups):
    rows = parts.shape[2]
    for n in range(size):
        for g in range(groups):
            for t in range(2):
                out, at = (outs[t], 0) if g == 0 else (outs[1 + g], t * size * rows)
                out[at + n * rows : at + (n + 1) * rows, :] = parts[n, 2 * g + t]


def to_heads(keys, values, groups):
    size = lax.axis_size("kvh")
    rows = keys.shape[0]
    vmem = pl.BlockSpec(memory_space=pltpu.VMEM)
    parts = pl.pallas_call(
        functools.partial(cut_kernel, size=size, groups=groups),
        in_specs=[vmem, vmem],
        out_specs=vmem,
        out_shape=jax.ShapeDtypeStruct((size, 2 * groups, rows, HD), keys.dtype),
        cost_estimate=COST,
        name="cut_heads",
    )(keys, values)
    parts = lax.all_to_all(parts, "kvh", split_axis=0, concat_axis=0, tiled=True)
    shapes = [(size * rows, HD)] * 2 + [(2 * size * rows, HD)] * (groups - 1)
    return pl.pallas_call(
        functools.partial(join_kernel, size=size, groups=groups),
        in_specs=[vmem],
        out_specs=[vmem] * len(shapes),
        out_shape=[jax.ShapeDtypeStruct(shape, keys.dtype) for shape in shapes],
        cost_estimate=COST,
        name="join_heads",
    )(parts)


def to_tokens(array, count):
    size = lax.axis_size("kvh")
    parts = jnp.moveaxis(array.reshape(count, size, -1, HD), 1, 0)
    parts = lax.all_to_all(parts, "kvh", split_axis=0, concat_axis=0, tiled=True)
    return [parts[:, t] for t in range(count)]


def per_device(queries, keys, values, out_grad, random_blocks):
    kvh = lax.axis_size("kvh")
    groups = keys.shape[1] // (kvh * HD)
    qpk = queries.shape[1] // (groups * HD)
    plan = Plan(lax.axis_size("ctx"), queries.shape[0] // BLK, random_blocks.shape[1])
    lanes, depth, qb = plan.lanes, plan.depth, plan.qb
    where = lax.axis_index("ctx").astype(jnp.int32).reshape(1)
    table, walk = tables(plan, where, random_blocks.reshape(-1))

    def spread(own):
        return [own] + [column_shift(own, plan, k) for k in range(1, depth)]

    def across(units, waits=()):
        return [row_shift(pack(plan, walk, units, lanes - t, waits), plan, lanes - t) for t in range(1, lanes)]

    def straight(units, waits=()):
        if plan.direct is None:
            return None
        return straight_shift(pack(plan, walk, units, 0, waits), plan, plan.direct, 0)

    def send_back(packs):
        return [row_shift(packs[t - 1], plan, t) for t in range(1, lanes)][::-1]

    def home(terms, count):
        arrived = [column_shift(terms[k], plan, depth - k) for k in range(1, depth)]
        total = terms[0]
        for array in arrived:
            total = total + array.astype(jnp.float32)
        return to_tokens(total.astype(jnp.bfloat16), count), arrived

    rows, size = qb * BLK, plan.slots * BLK
    own = to_heads(keys, values, groups)
    own, joined = own[:2], own[2:]
    units = [spread(a) for a in own]
    in_row = [[a] + [row_shift(a, plan, lanes - t) for t in range(1, lanes)] for a in joined]
    packs = [across([units[0]], tuple(a for some in in_row for a in some[1:]))]
    packs.append(across([units[1]], tuple(packs[0])))
    direct = straight([[a] for a in own], tuple(units[1][1:]))
    pieces = [(a, t, rows) for t in range(2) for a in units[t]] + [(a, t, size) for t in range(2) for a in packs[t]]
    if direct is not None:
        pieces.append((direct, 2, plan.direct_slots * BLK))
    ready = [a for unit in units for a in unit[1:]]
    found, homes, outs, arrived, waits = table, [], [], [], ()
    if groups > 1:
        row_found, row_walk = row_tables(plan, where, random_blocks.reshape(-1))
    for g in range(groups):
        last = g + 1 == groups
        if not last:
            sent = pack_rows(plan, row_walk, in_row[g], tuple(ready))
            waits = (sent[0],)
            ready = [column_shift(a, plan, step) for a, step in zip(sent, plan.row_slots)]
        run = functools.partial(attend, plan, found, table, queries, out_grad, pieces, g, qpk)
        if not g:
            outs, columns, (far, far_direct) = run(outs, True, 0, qb, (), waits)
        else:
            before = merge(plan, walk, *before, waits=tuple(a for a, _, _ in pieces))
            total, arrived = home(before, 2)
            homes.append(total)
            outs, columns, (far, far_direct) = run(outs, True, 0, qb, (), (before[1],))
        if arrived:
            far[1] = [gate(a, *arrived) for a in far[1]]
            far_direct = far_direct if far_direct is None else gate(far_direct, *arrived)
        if far_direct is not None:
            far_direct = straight_shift(far_direct, plan, 0, plan.direct)
        backs = [send_back(some) for some in far]
        if last:
            for t in range(2):
                terms = merge(plan, walk, [columns[t]], [backs[t]], far_direct, direct_first=t)
                homes.append(home(terms, 1)[0])
        else:
            before = columns, backs, far_direct
            found, pieces = row_found, [(a, 2, rows) for a in in_row[g]]
            pieces += [(a, 2, slots * BLK) for a, slots in zip(ready, plan.row_slots.values())]
    homes[-2:] = [homes[-2] + homes[-1]]
    key_grad, value_grad = (
        jnp.stack([some[n] for some in homes], axis=2).transpose(1, 0, 2, 3).reshape(keys.shape) for n in range(2)
    )
    return outs[0], outs[1], key_grad, value_grad


def solution(mesh):
    split = P("ctx", "kvh")
    home = P(("ctx", "kvh"), None)
    return jax.shard_map(
        per_device,
        mesh=mesh,
        in_specs=(split, home, home, split, P()),
        out_specs=(split, split, home, home),
        check_vma=False,
    )
```
